256 devices in a mesh: dp: 8 (over y_lo, x), tensor: 32 (over y_hi, z, core).
Axes of the slice: x: 4, y: 4 (y_hi: 2, y_lo: 2; y = y_hi * 2 + y_lo), z: 8, core: 2. Of those that a mesh axis runs over, the one named last changes fastest.
Arguments:
- inputs: bfloat16 [4096, 4096], P('dp', 'tensor'), may hold values from -6 to 6
- output_cotangent: bfloat16 [4096, 4096], P('dp', 'tensor'), may hold values from -6 to 6
- gate_frozen_weight: bfloat16 [4096, 16384], P(None, 'tensor'), may hold values from -0.1875 to 0.1875
- up_frozen_weight: bfloat16 [4096, 16384], P(None, 'tensor'), may hold values from -0.1875 to 0.1875
- down_frozen_weight: bfloat16 [16384, 4096], P('tensor'), may hold values from -0.046875 to 0.046875
- gate_input_factor: bfloat16 [32, 4096], P(None, 'tensor'), may hold values from -0.09375 to 0.09375
- gate_output_factor: bfloat16 [32, 16384], P(None, 'tensor'), may hold values from -0.875 to 0.875
- up_input_factor: bfloat16 [32, 4096], P(None, 'tensor'), may hold values from -0.09375 to 0.09375
- up_output_factor: bfloat16 [32, 16384], P(None, 'tensor'), may hold values from -0.875 to 0.875
- down_input_factor: bfloat16 [32, 16384], P(None, 'tensor'), may hold values from -0.09375 to 0.09375
- down_output_factor: bfloat16 [32, 4096], P(None, 'tensor'), may hold values from -0.875 to 0.875
Outputs:
- input_rows_gradient: bfloat16 [4096, 4096], P('dp', 'tensor')
- gate_input_factor_gradient: float32 [32, 4096], P(None, 'tensor')
- gate_output_factor_gradient: float32 [32, 16384], P(None, 'tensor')
- up_input_factor_gradient: float32 [32, 4096], P(None, 'tensor')
- up_output_factor_gradient: float32 [32, 16384], P(None, 'tensor')
- down_input_factor_gradient: float32 [32, 16384], P(None, 'tensor')
- down_output_factor_gradient: float32 [32, 4096], P(None, 'tensor')
The draws below stay inside these ranges and needn't reach their ends.
All inputs are finite; a program needn't handle non-finite values.
Results may differ from the reference program's by a relative error of at most 0.0055.
Values may be sent and summed in bfloat16 or wider, within the bound.
No kernel may reach another device: no remote copies, remote signals or barrier semaphores. Data moves between devices by JAX's collectives and lax.ppermute only.
A program may use at most 64 MiB of HBM per device.

```python
import jax
import jax.numpy as jnp
from jax import lax

MODEL_WIDTH = 4096
HIDDEN_UNITS = 16384
ADAPTER_RANK = 32
ROWS = 4096


def spiked(entries, stream_key, source, target, blocks, factor):
    def block_of(axis_at):
        return (jnp.arange(entries.shape[axis_at]) // (entries.shape[axis_at] // blocks)).reshape((-1,) + (1,) * (entries.ndim - 1 - axis_at))

    first = jax.random.permutation(stream_key, blocks)[block_of(target)]
    far = (block_of(target) + blocks // 2) % blocks
    return jnp.where((block_of(source) == first) | (block_of(source) == far), factor * entries, entries)


def shard_levels(stream_key, extent, cuts, smallest, top_value):
    def one(dim, parts):
        heights = jax.random.uniform(jax.random.fold_in(jax.random.fold_in(stream_key, 6), dim), (parts,), jnp.float32, smallest / len(cuts), top_value / len(cuts))
        return jnp.repeat(jnp.exp(heights), extent[dim] // parts).reshape((-1,) + (1,) * (len(extent) - dim - 1))

    level = one(*cuts[0])
    for cut in cuts[1:]:
        level = level * one(*cut)
    return level


def centred(rng, dims, width, reach, split=(), held_as=jnp.bfloat16):
    array = width * jax.random.normal(rng, dims, jnp.float32)
    if split:
        array = array * shard_levels(rng, dims, split, -0.22, 0.18)
    return jnp.clip(array, -reach, reach).astype(held_as)


def bell_draw_with(stream_key, extent, deviation, limit, cuts, heavy, kind=jnp.bfloat16):
    values = deviation * jax.random.normal(stream_key, extent, jnp.float32)
    if cuts:
        values = values * shard_levels(stream_key, extent, cuts, -0.22, 0.18)
    return jnp.clip(spiked(values, jax.random.fold_in(stream_key, 3), *heavy), -limit, limit).astype(kind)


def setup_inputs(seed: int = 0) -> dict:
    seeds = jax.random.split(jax.random.key(seed), 12)
    inputs = centred(seeds[0], (ROWS, MODEL_WIDTH), 1.0, 6.0, ((0, 8), (1, 32)))
    output_cotangent = centred(seeds[1], (ROWS, MODEL_WIDTH), 1.0, 6.0, ((0, 8), (1, 32)))
    gate_frozen_weight = bell_draw_with(seeds[2], (MODEL_WIDTH, HIDDEN_UNITS), MODEL_WIDTH ** -0.5, 0.1875, ((1, 32),), (1, 0, 32, 2.75))
    up_frozen_weight = bell_draw_with(seeds[3], (MODEL_WIDTH, HIDDEN_UNITS), MODEL_WIDTH ** -0.5, 0.1875, ((1, 32),), (1, 0, 32, 2.75))
    down_frozen_weight = centred(seeds[4], (HIDDEN_UNITS, MODEL_WIDTH), HIDDEN_UNITS ** -0.5, 0.046875, ((0, 32),))
    gate_input_factor = centred(seeds[5], (ADAPTER_RANK, MODEL_WIDTH), MODEL_WIDTH ** -0.5, 0.09375, ((1, 32),))
    gate_output_factor = centred(seeds[6], (ADAPTER_RANK, HIDDEN_UNITS), 50 ** -0.5, 0.875, ((1, 32),))
    up_input_factor = centred(seeds[7], (ADAPTER_RANK, MODEL_WIDTH), MODEL_WIDTH ** -0.5, 0.09375, ((1, 32),))
    up_output_factor = centred(seeds[8], (ADAPTER_RANK, HIDDEN_UNITS), 50 ** -0.5, 0.875, ((1, 32),))
    down_input_factor = centred(seeds[9], (ADAPTER_RANK, HIDDEN_UNITS), (HIDDEN_UNITS // 4) ** -0.5, 0.09375, ((1, 32),))
    down_output_factor = centred(seeds[10], (ADAPTER_RANK, MODEL_WIDTH), 50 ** -0.5, 0.875, ((1, 32),))
    return dict(inputs=inputs, output_cotangent=output_cotangent, gate_frozen_weight=gate_frozen_weight, up_frozen_weight=up_frozen_weight, down_frozen_weight=down_frozen_weight, gate_input_factor=gate_input_factor, gate_output_factor=gate_output_factor, up_input_factor=up_input_factor, up_output_factor=up_output_factor, down_input_factor=down_input_factor, down_output_factor=down_output_factor)


adapter_scale = 0.5


def contract_trailing(left, right):
    return lax.dot_general(left, right, (((1,), (1,)), ((), ())), preferred_element_type=jnp.float32)


def contract_leading(left, right):
    return lax.dot_general(left, right, (((0,), (0,)), ((), ())), preferred_element_type=jnp.float32)


def reference(inputs, output_cotangent, gate_frozen_weight, up_frozen_weight, down_frozen_weight, gate_input_factor, gate_output_factor, up_input_factor, up_output_factor, down_input_factor, down_output_factor):
    gate_narrow_input = contract_trailing(inputs, gate_input_factor).astype(jnp.bfloat16)
    up_narrow_input = contract_trailing(inputs, up_input_factor).astype(jnp.bfloat16)
    cotangent_narrow = contract_trailing(output_cotangent, down_output_factor).astype(jnp.bfloat16)
    gate_preactivation = jnp.dot(inputs, gate_frozen_weight, preferred_element_type=jnp.float32) + adapter_scale * jnp.dot(gate_narrow_input, gate_output_factor, preferred_element_type=jnp.float32)
    up_preactivation = jnp.dot(inputs, up_frozen_weight, preferred_element_type=jnp.float32) + adapter_scale * jnp.dot(up_narrow_input, up_output_factor, preferred_element_type=jnp.float32)
    sigmoid_gate = jax.nn.sigmoid(gate_preactivation)
    activated = gate_preactivation * sigmoid_gate
    hidden_activation = (activated * up_preactivation).astype(jnp.bfloat16)
    hidden_narrow = contract_trailing(hidden_activation, down_input_factor).astype(jnp.bfloat16)
    hidden_gradient = contract_trailing(output_cotangent, down_frozen_weight) + adapter_scale * jnp.dot(cotangent_narrow, down_input_factor, preferred_element_type=jnp.float32)
    gate_activation_gradient = (hidden_gradient * up_preactivation * sigmoid_gate * (1.0 + gate_preactivation * (1.0 - sigmoid_gate))).astype(jnp.bfloat16)
    up_activation_gradient = (hidden_gradient * activated).astype(jnp.bfloat16)
    gate_narrow_output = contract_trailing(gate_activation_gradient, gate_output_factor).astype(jnp.bfloat16)
    up_narrow_output = contract_trailing(up_activation_gradient, up_output_factor).astype(jnp.bfloat16)
    input_rows_gradient = contract_trailing(gate_activation_gradient, gate_frozen_weight) + contract_trailing(up_activation_gradient, up_frozen_weight)
    input_rows_gradient = input_rows_gradient + adapter_scale * (jnp.dot(gate_narrow_output, gate_input_factor, preferred_element_type=jnp.float32) + jnp.dot(up_narrow_output, up_input_factor, preferred_element_type=jnp.float32))
    input_rows_gradient = input_rows_gradient.astype(jnp.bfloat16)
    gate_input_factor_gradient = adapter_scale * contract_leading(gate_narrow_output, inputs)
    gate_output_factor_gradient = adapter_scale * contract_leading(gate_narrow_input, gate_activation_gradient)
    up_input_factor_gradient = adapter_scale * contract_leading(up_narrow_output, inputs)
    up_output_factor_gradient = adapter_scale * contract_leading(up_narrow_input, up_activation_gradient)
    down_input_factor_gradient = adapter_scale * contract_leading(cotangent_narrow, hidden_activation)
    down_output_factor_gradient = adapter_scale * contract_leading(hidden_narrow, output_cotangent)
    return (input_rows_gradient, gate_input_factor_gradient, gate_output_factor_gradient, up_input_factor_gradient, up_output_factor_gradient, down_input_factor_gradient, down_output_factor_gradient)
```

```python
import functools

import jax
import jax.numpy as jnp
from jax import lax
from jax.experimental import pallas as pl
from jax.experimental.pallas import tpu as pltpu
from jax.sharding import Mesh, PartitionSpec as P

SCALE = 0.5
ROWS = 512
LANES = 128
HID = 512
RANK = 32
RANKS = 3 * RANK
PIECE = 2 * ROWS + RANKS
ZN = 8
VMEM_LIMIT = 48 * 1024 * 1024
F32 = jnp.float32
BF16 = jnp.bfloat16

VM = pl.BlockSpec(memory_space=pltpu.VMEM)
SM = pl.BlockSpec(memory_space=pltpu.SMEM)
HB = pl.BlockSpec(memory_space=pl.ANY)


def dot_nn(a, b):
    return lax.dot_general(a, b, (((1,), (0,)), ((), ())), preferred_element_type=F32)


def dot_nt(a, b):
    return lax.dot_general(a, b, (((1,), (1,)), ((), ())), preferred_element_type=F32)


def dot_tn(a, b):
    return lax.dot_general(a, b, (((0,), (0,)), ((), ())), preferred_element_type=F32)


def block_index(idx, k, r, other):
    yhi = lax.rem(idx[0] + r, 2)
    z = lax.rem(idx[1] + (k + ZN), ZN)
    c = lax.rem(idx[2] + other, 2)
    return yhi * 16 + z * 2 + c


def weight_copies(idx, slot, k, wg, wu, wd, bg, bu, bd, sem):
    copies = []
    for j in range(4):
        at = pl.multiple_of(block_index(idx, k, j // 2, j % 2) * LANES, LANES)
        cols = pl.ds(j * LANES, LANES)
        copies.append(
            [
                pltpu.make_async_copy(wg.at[pl.ds(at, LANES), :], bg.at[slot, cols, :], sem.at[slot, j, 0]),
                pltpu.make_async_copy(wu.at[pl.ds(at, LANES), :], bu.at[slot, cols, :], sem.at[slot, j, 1]),
                pltpu.make_async_copy(wd.at[:, pl.ds(at, LANES)], bd.at[slot, :, cols], sem.at[slot, j, 2]),
            ]
        )
    return [c for group in copies for c in group]


def accumulate(ks, first, idx, pieces, weights, accs, outs, bufs, sem):
    every = [weight_copies(idx, s, k, *weights, *bufs, sem) for s, k in enumerate(ks)]
    for group in every:
        for c in group:
            c.start()
    for s, _ in enumerate(ks):
        four = pieces[4 * s : 4 * s + 4]
        x = jnp.concatenate([p[0:ROWS, :] for p in four], axis=1)
        c = jnp.concatenate([p[ROWS : 2 * ROWS, :] for p in four], axis=1)
        f = jnp.concatenate([p[2 * ROWS : PIECE, :] for p in four], axis=1)
        for copy in every[s]:
            copy.wait()
        new = (
            dot_nn(x, bufs[0][s]),
            dot_nn(x, bufs[1][s]),
            dot_nt(c, bufs[2][s]),
        )
        ranks = (dot_nt(f[0 : 2 * RANK], x), dot_nt(f[2 * RANK : RANKS], c))
        fresh = first and s == 0
        src = accs if s == 0 else outs
        for i in range(3):
            outs[i][...] = new[i] if fresh else src[i][...] + new[i]
        for lo, hi, val in ((0, 2 * RANK, ranks[0]), (2 * RANK, RANKS, ranks[1])):
            outs[3][lo:hi, :] = val if fresh else src[3][lo:hi, :] + val


def acc_kernel(ks, first, *refs):
    refs = list(refs)
    idx = refs.pop(0)
    n = 4 * len(ks)
    pieces, refs = refs[:n], refs[n:]
    weights, refs = refs[:3], refs[3:]
    accs = None
    if not first:
        accs, refs = refs[:4], refs[4:]
    outs, refs = refs[:4], refs[4:]
    bufs, sem = refs[:3], refs[3]
    accumulate(ks, first, idx, pieces, weights, accs, outs, bufs, sem)


def weight_scratch(n):
    return [
        pltpu.VMEM((n, HID, HID), BF16),
        pltpu.VMEM((n, HID, HID), BF16),
        pltpu.VMEM((n, HID, HID), BF16),
        pltpu.SemaphoreType.DMA((n, 4, 3)),
    ]


ACC_SHAPES = [jax.ShapeDtypeStruct((ROWS, HID), F32)] * 3 + [jax.ShapeDtypeStruct((RANKS, ROWS), F32)]


def params():
    return pltpu.CompilerParams(vmem_limit_bytes=VMEM_LIMIT)


def run_acc(ks, idx, pieces, weights, accs):
    first = accs is None
    args = [idx, *pieces, *weights] + ([] if first else list(accs))
    specs = [SM] + [VM] * len(pieces) + [HB] * 3 + ([] if first else [VM] * 4)
    aliases = {} if first else {len(args) - 4 + i: i for i in range(4)}
    return pl.pallas_call(
        functools.partial(acc_kernel, ks, first),
        out_shape=ACC_SHAPES,
        in_specs=specs,
        out_specs=[VM] * 4,
        scratch_shapes=weight_scratch(len(ks)),
        input_output_aliases=aliases,
        compiler_params=params(),
        cost_estimate=pl.CostEstimate(
            flops=len(ks) * 2 * ROWS * HID * HID * 4, bytes_accessed=len(ks) * 3 * 2**20, transcendentals=0
        ),
    )(*args)


def mid_kernel(ks, *refs):
    refs = list(refs)
    idx = refs.pop(0)
    n = 4 * len(ks)
    pieces, refs = refs[:n], refs[n:]
    weights, refs = refs[:3], refs[3:]
    accs, refs = refs[:4], refs[4:]
    gof, uof, dif = refs[:3]
    out, grads = refs[3:5]
    g, u, h, rt, hid = refs[5:10]
    bufs, sem = refs[10:13], refs[13]
    accumulate(ks, False, idx, pieces, weights, accs, (g, u, h, rt), bufs, sem)
    ranks = rt[...].astype(BF16)
    g[...] += SCALE * dot_tn(ranks[0:RANK], gof[...])
    u[...] += SCALE * dot_tn(ranks[RANK : 2 * RANK], uof[...])
    h[...] += SCALE * dot_tn(ranks[2 * RANK : RANKS], dif[...])
    step = 64

    @pl.loop(0, ROWS // step)
    def _(i):
        at = pl.ds(pl.multiple_of(i * step, step), step)
        gate, up, grad = g[at, :], u[at, :], h[at, :]
        sig = jax.nn.sigmoid(gate)
        act = gate * sig
        hid[at, :] = (act * up).astype(BF16)
        out[at, :] = (grad * up * sig * (1.0 + gate * (1.0 - sig))).astype(BF16)
        out[pl.ds(pl.multiple_of(ROWS + i * step, step), step), :] = (grad * act).astype(BF16)

    gg, ug, hd = out[0:ROWS, :], out[ROWS : 2 * ROWS, :], hid[...]
    base = 2 * ROWS
    out[base : base + RANK, :] = dot_nt(gof[...], gg).astype(BF16)
    out[base + RANK : base + 2 * RANK, :] = dot_nt(uof[...], ug).astype(BF16)
    out[base + 2 * RANK : PIECE, :] = dot_nt(dif[...], hd).astype(BF16)
    grads[0:RANK, :] = SCALE * dot_nn(ranks[0:RANK], gg)
    grads[RANK : 2 * RANK, :] = SCALE * dot_nn(ranks[RANK : 2 * RANK], ug)
    grads[2 * RANK : RANKS, :] = SCALE * dot_nn(ranks[2 * RANK : RANKS], hd)


def run_mid(ks, idx, pieces, weights, accs, factors):
    args = [idx, *pieces, *weights, *accs, *factors]
    return pl.pallas_call(
        functools.partial(mid_kernel, ks),
        out_shape=[jax.ShapeDtypeStruct((PIECE, HID), BF16), jax.ShapeDtypeStruct((RANKS, HID), F32)],
        in_specs=[SM] + [VM] * len(pieces) + [HB] * 3 + [VM] * 7,
        out_specs=[VM] * 2,
        scratch_shapes=[
            pltpu.VMEM((ROWS, HID), F32),
            pltpu.VMEM((ROWS, HID), F32),
            pltpu.VMEM((ROWS, HID), F32),
            pltpu.VMEM((RANKS, ROWS), F32),
            pltpu.VMEM((ROWS, HID), BF16),
        ]
        + weight_scratch(len(ks)),
        compiler_params=params(),
        cost_estimate=pl.CostEstimate(
            flops=(len(ks) * 4 + 4) * 2 * ROWS * HID * HID, bytes_accessed=4 * 2**20, transcendentals=ROWS * HID
        ),
    )(*args)


def out_kernel(ks, kinds, *refs):
    refs = list(refs)
    idx, mine, theirs = refs[:3]
    refs = refs[3:]
    pieces, refs = refs[: 2 * len(ks)], refs[2 * len(ks) :]
    wg, wu, wp = refs[:3]
    outs = refs[3 : 3 + 2 * len(ks)]
    wb, sem = refs[3 + 2 * len(ks) :]
    every = []
    for s, k in enumerate(ks):
        group = []
        for r in range(2):
            fb = block_index(idx, k, r, 0)
            at = pl.multiple_of(fb * LANES, LANES)
            half = fb // 2
            rows = pl.ds(r * LANES, LANES)
            group += [
                pltpu.make_async_copy(wg.at[pl.ds(at, LANES), :], wb.at[s, 0, rows, :], sem.at[s, r, 0]),
                pltpu.make_async_copy(wu.at[pl.ds(at, LANES), :], wb.at[s, 1, rows, :], sem.at[s, r, 1]),
                pltpu.make_async_copy(wp.at[0, half], wb.at[s, 2, rows, :], sem.at[s, r, 2]),
                pltpu.make_async_copy(wp.at[1, half], wb.at[s, 3, rows, :], sem.at[s, r, 3]),
            ]
        every.append(group)
    for group in every:
        for c in group:
            c.start()
    ranks = (mine[2 * ROWS : PIECE, :].astype(F32) + theirs[2 * ROWS : PIECE, :].astype(F32)).astype(BF16)
    wide = jnp.concatenate(
        [mine[0:ROWS, :], mine[ROWS : 2 * ROWS, :], theirs[0:ROWS, :], theirs[ROWS : 2 * ROWS, :]], axis=1
    )
    for s, _ in enumerate(ks):
        two = pieces[2 * s : 2 * s + 2]
        x = jnp.concatenate([p[0:ROWS, :] for p in two], axis=1)
        c = jnp.concatenate([p[ROWS : 2 * ROWS, :] for p in two], axis=1)
        f = jnp.concatenate([p[2 * ROWS : 2 * ROWS + 2 * RANK, :] for p in two], axis=1)
        adapter = SCALE * dot_tn(ranks[0 : 2 * RANK], f)
        grad_x = dot_nn(ranks[0 : 2 * RANK], x)
        grad_c = dot_nn(ranks[2 * RANK : RANKS], c)
        for copy in every[s]:
            copy.wait()
        w = jnp.concatenate([wb[s, i] for i in range(4)], axis=1)
        rows = dot_nt(wide, w) + adapter
        for r in range(2):
            o = outs[2 * s + r]
            lanes = slice(r * LANES, (r + 1) * LANES)
            o[0:ROWS, :] = rows[:, lanes].astype(o.dtype)
            o[ROWS : ROWS + 2 * RANK, :] = grad_x[:, lanes].astype(o.dtype)
            o[ROWS + 2 * RANK : ROWS + RANKS, :] = grad_c[:, lanes].astype(o.dtype)


def run_out(ks, kinds, idx, mine, theirs, pieces, weights):
    n = len(ks)
    return pl.pallas_call(
        functools.partial(out_kernel, ks, kinds),
        out_shape=[jax.ShapeDtypeStruct((ROWS + RANKS, LANES), kind) for kind in kinds],
        in_specs=[SM, VM, VM] + [VM] * (2 * n) + [HB] * 3,
        out_specs=[VM] * (2 * n),
        scratch_shapes=[pltpu.VMEM((n, 4, 2 * LANES, HID), BF16), pltpu.SemaphoreType.DMA((n, 2, 4))],
        compiler_params=params(),
        cost_estimate=pl.CostEstimate(
            flops=n * 2 * ROWS * 2 * LANES * 4 * HID, bytes_accessed=n * 2**20, transcendentals=0
        ),
    )(idx, mine, theirs, *pieces, *weights)


def shift(v, axis, n, by):
    return lax.ppermute(v, axis, [(i, (i + by) % n) for i in range(n)])


def flip(v, axis, n, bits):
    return lax.ppermute(v, axis, [(i, i ^ bits) for i in range(n)])


def up(v):
    return shift(v, "z", ZN, 1)


def down(v):
    return shift(v, "z", ZN, ZN - 1)


def sum_rows(v):
    pair = v + flip(v, "x", 4, 1)
    far = flip(v, "x", 4, 2) + flip(v, "x", 4, 3)
    quad = pair + far
    return quad + flip(quad, "ylo", 2, 1)


def body(x, dy, wg, wu, wd, gif, gof, uif, uof, dif, dof):
    yhi, z, core = lax.axis_index("yhi"), lax.axis_index("z"), lax.axis_index("core")
    idx = jnp.stack([yhi, z, core]).astype(jnp.int32)

    a0 = jnp.concatenate([x, dy, gif, uif, dof], axis=0)
    b0 = flip(a0, "yhi", 2, 1)
    mine = {0: (a0, b0)}
    ua, da = [a0], [a0]
    ub, db = [b0], [b0]
    for j in range(1, 5):
        ua.append(up(ua[-1]))
        if j < 4:
            da.append(down(da[-1]))
            ub.append(up(ub[-1]))
        db.append(down(db[-1]))
        if j < 4:
            mine[-j] = (ua[j], ub[j])
            mine[j] = (da[j], db[j])
    mine[4] = (ua[4], db[4])

    def select(w):
        return lax.dynamic_index_in_dim(w.reshape(16, 2, LANES, HID), 1 - core, 1, keepdims=False)

    wp = flip(jnp.stack([select(wg), select(wu)]), "core", 2, 1)

    def four(k):
        a, b = mine[k]
        return [a, flip(a, "core", 2, 1), b, flip(b, "core", 2, 1)]

    def group(ks):
        return [p for k in ks for p in four(k)]

    weights = (wg, wu, wd)
    accs = None
    for ks in ((0,), (-1, 1), (-2, 2), (-3, 3)):
        accs = run_acc(ks, idx, group(ks), weights, accs)
    sent, grads = run_mid((4,), idx, group((4,)), weights, accs, (gof, uof, dif))
    got = flip(sent, "core", 2, 1)

    def two(ks):
        return [p for k in ks for p in mine[k]]

    ow = (wg, wu, wp)
    k1 = (4, 3, -3)
    r1 = run_out(k1, (BF16, BF16, F32, BF16, BF16, F32), idx, sent, got, two(k1), ow)
    k2 = (2, -2, 1, -1, 0)
    r2 = run_out(k2, (F32,) * 10, idx, sent, got, two(k2), ow)
    pa = {k: r1[2 * i] for i, k in enumerate(k1)} | {k: r2[2 * i] for i, k in enumerate(k2)}
    pb = {k: r1[2 * i + 1] for i, k in enumerate(k1)} | {k: r2[2 * i + 1] for i, k in enumerate(k2)}

    def join(moving, own):
        return (moving.astype(F32) + own).astype(BF16)

    sa, sb = up(pa[4]), down(pb[4])
    tb, ta = up(pb[3]), down(pa[-3])
    for k in (3, 2, 1):
        sa, sb = up(join(sa, pa[k])), down(join(sb, pb[-k]))
        if k > 1:
            tb, ta = up(join(tb, pb[k - 1])), down(join(ta, pa[-(k - 1)]))
    total_a = pa[0] + sa.astype(F32) + ta.astype(F32)
    total_b = pb[0] + sb.astype(F32) + tb.astype(F32)
    total = total_a + flip(total_b.astype(BF16), "yhi", 2, 1).astype(F32)
    rows_grad = total[0:ROWS].astype(BF16)
    in_grads = SCALE * sum_rows(total[ROWS : ROWS + RANKS])
    out_grads = sum_rows(grads)
    g = [in_grads[i * RANK : (i + 1) * RANK] for i in range(3)]
    o = [out_grads[i * RANK : (i + 1) * RANK] for i in range(3)]
    return rows_grad, g[0], o[0], g[1], o[1], o[2], g[2]


def solution(mesh):
    split = Mesh(mesh.devices.reshape(2, 4, 2, 8, 2), ("ylo", "x", "yhi", "z", "core"))
    dp, tensor = ("ylo", "x"), ("yhi", "z", "core")
    cols = P(None, tensor)
    return jax.shard_map(
        body,
        mesh=split,
        in_specs=(P(dp, tensor), P(dp, tensor), cols, cols, P(tensor, None), cols, cols, cols, cols, cols, cols),
        out_specs=(P(dp, tensor), cols, cols, cols, cols, cols, cols),
        check_vma=False,
    )
```

```python
import functools

import jax
import jax.numpy as jnp
from jax import lax
from jax.experimental import pallas as pl
from jax.experimental.pallas import tpu as pltpu
from jax.sharding import Mesh, PartitionSpec as P

SCALE = 0.5
ROWS = 512
HALF = ROWS // 2
LANES = 128
FEATS = 2 * LANES
HID = 512
WIDE = 2 * HID
RANK = 32
RANKS = 3 * RANK
PIECE = 2 * HALF + RANKS
ZN = 8
VMEM_LIMIT = 24 * 1024 * 1024
F32 = jnp.float32
BF16 = jnp.bfloat16

VM = pl.BlockSpec(memory_space=pltpu.VMEM)
SM = pl.BlockSpec(memory_space=pltpu.SMEM)
HB = pl.BlockSpec(memory_space=pltpu.HBM)


def dot_nn(a, b):
    return lax.dot_general(a, b, (((1,), (0,)), ((), ())), preferred_element_type=F32)


def dot_nt(a, b):
    return lax.dot_general(a, b, (((1,), (1,)), ((), ())), preferred_element_type=F32)


def dot_tn(a, b):
    return lax.dot_general(a, b, (((0,), (0,)), ((), ())), preferred_element_type=F32)


def feature_at(idx, k, r):
    yhi = lax.rem(idx[0] + r, 2)
    z = lax.rem(idx[1] + (k + ZN), ZN)
    return pl.multiple_of((yhi * ZN + z) * FEATS, FEATS)


def up_copies(idx, slot, k, wg, wu, wgp, wup, bg, bu, sem):
    gate, up = [], []
    for r in range(2):
        at = pl.ds(feature_at(idx, k, r), FEATS)
        rows = pl.ds(r * FEATS, FEATS)
        for o, (g, u) in enumerate(((wg, wu), (wgp, wup))):
            lanes = pl.ds(o * HID, HID)
            gate.append(pltpu.make_async_copy(g.at[at, :], bg.at[slot, rows, lanes], sem.at[slot, r, o, 0]))
            up.append(pltpu.make_async_copy(u.at[at, :], bu.at[slot, rows, lanes], sem.at[slot, r, o, 1]))
    return gate, up


def down_copies(idx, slot, k, wd, wdp, bd, sem):
    down = []
    for r in range(2):
        at = pl.ds(feature_at(idx, k, r), FEATS)
        for o, d in enumerate((wd, wdp)):
            down.append(
                pltpu.make_async_copy(
                    d.at[:, at], bd.at[slot, pl.ds(o * HID, HID), pl.ds(r * FEATS, FEATS)], sem.at[slot, r, o, 2]
                )
            )
    return down


def wait_all(copies):
    for c in copies:
        c.wait()


def accumulate(ks, first, idx, pieces, weights, accs, outs, bufs, sem):
    wg, wu, wd, wgp, wup, wdp = weights
    bg, bu, bd = bufs
    every = []
    for s, k in enumerate(ks):
        gate, upw = up_copies(idx, s, k, wg, wu, wgp, wup, bg, bu, sem)
        every.append((gate, upw, down_copies(idx, s, k, wd, wdp, bd, sem)))
        for group in every[-1]:
            for c in group:
                c.start()
    for s, _ in enumerate(ks):
        two = pieces[2 * s : 2 * s + 2]
        x, c, f = (
            jnp.concatenate([p[lo:hi, :] for p in two], axis=1)
            for lo, hi in ((0, HALF), (HALF, 2 * HALF), (2 * HALF, PIECE))
        )
        fresh = first and s == 0
        src = accs if s == 0 else outs

        def put(i, at, val):
            outs[i][at] = val if fresh else src[i][at] + val

        put(3, (slice(0, 2 * RANK), slice(None)), dot_nt(f[0 : 2 * RANK], x))
        put(3, (slice(2 * RANK, RANKS), slice(None)), dot_nt(f[2 * RANK : RANKS], c))
        wait_all(every[s][0])
        put(0, Ellipsis, dot_nn(x, bg[s]))
        wait_all(every[s][1])
        put(1, Ellipsis, dot_nn(x, bu[s]))
        wait_all(every[s][2])
        put(2, Ellipsis, dot_nt(c, bd[s]))


def acc_kernel(ks, first, *refs):
    refs = list(refs)
    idx = refs.pop(0)
    n = 2 * len(ks)
    pieces, refs = refs[:n], refs[n:]
    weights, refs = refs[:6], refs[6:]
    accs = None
    if not first:
        accs, refs = refs[:4], refs[4:]
    outs, bufs, sem = refs[:4], refs[4:7], refs[7]
    accumulate(ks, first, idx, pieces, weights, accs, outs, bufs, sem)


def weight_scratch(n):
    return [
        pltpu.VMEM((n, 2 * FEATS, WIDE), BF16),
        pltpu.VMEM((n, 2 * FEATS, WIDE), BF16),
        pltpu.VMEM((n, WIDE, 2 * FEATS), BF16),
        pltpu.SemaphoreType.DMA((n, 2, 2, 3)),
    ]


ACC_SHAPES = [jax.ShapeDtypeStruct((HALF, WIDE), F32)] * 3 + [jax.ShapeDtypeStruct((RANKS, HALF), F32)]


def params():
    return pltpu.CompilerParams(vmem_limit_bytes=VMEM_LIMIT)


def run_acc(ks, idx, pieces, weights, accs):
    first = accs is None
    args = [idx, *pieces, *map(stay, weights)] + ([] if first else list(accs))
    specs = [SM] + [VM] * len(pieces) + [HB] * 6 + ([] if first else [VM] * 4)
    aliases = {} if first else {len(args) - 4 + i: i for i in range(4)}
    return pl.pallas_call(
        functools.partial(acc_kernel, ks, first),
        out_shape=ACC_SHAPES,
        in_specs=specs,
        out_specs=[VM] * 4,
        scratch_shapes=weight_scratch(len(ks)),
        input_output_aliases=aliases,
        compiler_params=params(),
        cost_estimate=pl.CostEstimate(
            flops=len(ks) * 2 * HALF * WIDE * HID * 4, bytes_accessed=len(ks) * 3 * 2**20, transcendentals=0
        ),
    )(*args)


def grad_block(wide, ranks, f, bg, bu):
    rows = dot_nt(wide[:, 0:WIDE], bg) + dot_nt(wide[:, WIDE : 2 * WIDE], bu)
    return rows + SCALE * dot_tn(ranks, f)


def two_factors(two):
    return jnp.concatenate([p[2 * HALF : 2 * HALF + 2 * RANK, :] for p in two], axis=1)


def mid_kernel(k, *refs):
    refs = list(refs)
    idx = refs.pop(0)
    pieces, refs = refs[:2], refs[2:]
    weights, refs = refs[:6], refs[6:]
    accs, refs = refs[:4], refs[4:]
    mine, theirs = refs[:2]
    wide, ranks_out, grads, oa, ob = refs[2:7]
    g, u, h, rt, hid = refs[7:12]
    bufs, sem = refs[12:15], refs[15]
    accumulate((k,), False, idx, pieces, weights, accs, (g, u, h, rt), bufs, sem)
    ranks = rt[...].astype(BF16)
    fac = jnp.concatenate([mine[...], theirs[...]], axis=1)
    for i, ref in enumerate((g, u, h)):
        at = slice(i * RANK, (i + 1) * RANK)
        ref[...] += SCALE * dot_tn(ranks[at], fac[at])
    step = 32

    @pl.loop(0, HALF // step)
    def _(i):
        at = pl.ds(pl.multiple_of(i * step, step), step)
        gate, up, grad = g[at, :], u[at, :], h[at, :]
        sig = jax.nn.sigmoid(gate)
        act = gate * sig
        hid[at, :] = (act * up).astype(BF16)
        wide[at, 0:WIDE] = (grad * up * sig * (1.0 + gate * (1.0 - sig))).astype(BF16)
        wide[at, WIDE : 2 * WIDE] = (grad * act).astype(BF16)

    three = (wide[:, 0:WIDE], wide[:, WIDE : 2 * WIDE], hid[...])
    for i, val in enumerate(three):
        at = slice(i * RANK, (i + 1) * RANK)
        ranks_out[at, :] = dot_nt(fac[at], val)
    two = ranks_out[0 : 2 * RANK, :].astype(BF16)
    rows = grad_block(wide[...], two, two_factors(pieces), bufs[0][0], bufs[1][0]).astype(BF16)
    oa[...] = rows[:, 0:FEATS]
    ob[...] = rows[:, FEATS : 2 * FEATS]
    for i, val in enumerate(three):
        at = slice(i * RANK, (i + 1) * RANK)
        grads[at, :] = SCALE * dot_nn(ranks[at], val)


def run_mid(k, idx, pieces, weights, accs, mine, theirs):
    block = jax.ShapeDtypeStruct((HALF, FEATS), BF16)
    return pl.pallas_call(
        functools.partial(mid_kernel, k),
        out_shape=[
            jax.ShapeDtypeStruct((HALF, 2 * WIDE), BF16),
            jax.ShapeDtypeStruct((RANKS, HALF), F32),
            jax.ShapeDtypeStruct((RANKS, WIDE), F32),
            block,
            block,
        ],
        in_specs=[SM] + [VM] * 2 + [HB] * 6 + [VM] * 6,
        out_specs=[VM] * 5,
        scratch_shapes=[
            pltpu.VMEM((HALF, WIDE), F32),
            pltpu.VMEM((HALF, WIDE), F32),
            pltpu.VMEM((HALF, WIDE), F32),
            pltpu.VMEM((RANKS, HALF), F32),
            pltpu.VMEM((HALF, WIDE), BF16),
        ]
        + weight_scratch(1),
        compiler_params=params(),
        cost_estimate=pl.CostEstimate(
            flops=8 * 2 * HALF * WIDE * HID, bytes_accessed=4 * 2**20, transcendentals=HALF * WIDE
        ),
    )(idx, *pieces, *map(stay, weights), *accs, mine, theirs)


def out_kernel(ks, *refs):
    refs = list(refs)
    idx, wide, ranks_out = refs[:3]
    refs = refs[3:]
    n = 2 * len(ks)
    pieces, refs = refs[:n], refs[n:]
    weights, refs = refs[:4], refs[4:]
    outs, (bg, bu, sem) = refs[:n], refs[n:]
    every = [up_copies(idx, s, k, *weights, bg, bu, sem) for s, k in enumerate(ks)]
    for gate, upw in every:
        for c in gate + upw:
            c.start()
    two = ranks_out[0 : 2 * RANK, :].astype(BF16)
    for s, _ in enumerate(ks):
        f = two_factors(pieces[2 * s : 2 * s + 2])
        wait_all(every[s][0] + every[s][1])
        rows = grad_block(wide[...], two, f, bg[s], bu[s])
        for r in range(2):
            o = outs[2 * s + r]
            o[...] = rows[:, r * FEATS : (r + 1) * FEATS].astype(o.dtype)


def run_out(ks, kinds, idx, wide, ranks_out, pieces, weights):
    n = len(ks)
    return pl.pallas_call(
        functools.partial(out_kernel, ks),
        out_shape=[jax.ShapeDtypeStruct((HALF, FEATS), kind) for kind in kinds],
        in_specs=[SM, VM, VM] + [VM] * (2 * n) + [HB] * 4,
        out_specs=[VM] * (2 * n),
        scratch_shapes=[
            pltpu.VMEM((n, 2 * FEATS, WIDE), BF16),
            pltpu.VMEM((n, 2 * FEATS, WIDE), BF16),
            pltpu.SemaphoreType.DMA((n, 2, 2, 2)),
        ],
        compiler_params=params(),
        cost_estimate=pl.CostEstimate(
            flops=n * 2 * HALF * 2 * FEATS * 2 * WIDE, bytes_accessed=n * 2 * 2**20, transcendentals=0
        ),
    )(idx, wide, ranks_out, *pieces, *map(stay, weights))


def shift(v, axis, n, by):
    return lax.ppermute(v, axis, [(i, (i + by) % n) for i in range(n)])


def flip(v, axis, n, bits):
    return lax.ppermute(v, axis, [(i, i ^ bits) for i in range(n)])


def up(v):
    return shift(v, "z", ZN, 1)


def down(v):
    return shift(v, "z", ZN, ZN - 1)


def stay(v):
    return pltpu.with_memory_space_constraint(v, pltpu.HBM)


def keep(v):
    return pltpu.with_memory_space_constraint(v, pltpu.VMEM)


def swap(v):
    return flip(v, "core", 2, 1)


def after(v, done):
    return lax.optimization_barrier((v, done))[0]


def ordered(core, mine, theirs, axis):
    first = core == 0
    return jnp.concatenate([jnp.where(first, mine, theirs), jnp.where(first, theirs, mine)], axis=axis)


def body(x, dy, wg, wu, wd, gif, gof, uif, uof, dif, dof):
    yhi, z, core = lax.axis_index("yhi"), lax.axis_index("z"), lax.axis_index("core")
    idx = jnp.stack([yhi, z, core]).astype(jnp.int32)

    def half(c):
        rows = [lax.dynamic_slice_in_dim(v, c * HALF, HALF) for v in (x, dy)]
        return jnp.concatenate(rows + [gif, uif, dof], axis=0)

    a0 = ordered(core, half(core), swap(half(1 - core)), 1)
    a0_, wg_, wu_, wd_, gof_, uof_, dif_ = lax.optimization_barrier((a0, wg, wu, wd, gof, uof, dif))
    b0 = flip(a0, "yhi", 2, 1)
    ua1, da1 = up(a0), down(a0)
    factors = jnp.concatenate([gof_, uof_, dif_], axis=0)
    their_factors = swap(factors)
    weights = (wg, wu, wd, swap(wg_), swap(wu_), swap(wd_))
    out_weights = (wg, wu, weights[3], weights[4])

    ub1, db1 = up(b0), down(b0)
    ua2, da2 = up(ua1), down(da1)
    accs = run_acc((0, -1, 1), idx, [a0, b0, ua1, ub1, da1, db1], weights, None)
    ub2, db2 = up(ub1), down(db1)
    ua3, da3 = up(ua2), down(da2)
    ub3, db3 = up(after(ub2, accs[3])), down(after(db2, accs[3]))
    accs = run_acc((-2, 2), idx, [ua2, ub2, da2, db2], weights, accs)
    ua4 = up(ua3)
    db4 = down(after(db3, accs[3]))
    accs = run_acc((-3, 3), idx, [ua3, ub3, da3, db3], weights, accs)
    mine = {0: (a0, b0), -1: (ua1, ub1), 1: (da1, db1), -2: (ua2, ub2), 2: (da2, db2), -3: (ua3, ub3), 3: (da3, db3)}
    wide, ranks_out, grads, a4, b4 = run_mid(4, idx, [ua4, db4], weights, accs, factors, their_factors)

    def two(ks):
        return [p for k in ks for p in mine[k]]

    sa, sb = up(a4), down(b4)
    k1 = (3, -3)
    r1 = run_out(k1, (F32, BF16, BF16, F32), idx, wide, ranks_out, two(k1), out_weights)
    tb, ta = up(r1[1]), down(r1[2])
    k2 = (2, -2, 1, -1, 0)
    r2 = run_out(k2, (F32,) * 10, idx, wide, ranks_out, two(k2), out_weights)
    pa = {3: r1[0]} | {k: r2[2 * i] for i, k in enumerate(k2)}
    pb = {-3: r1[3]} | {k: r2[2 * i + 1] for i, k in enumerate(k2)}

    def join(moving, own):
        return (moving.astype(F32) + own).astype(BF16)

    for k in (3, 2, 1):
        sa, sb = up(join(sa, pa[k])), down(join(sb, pb[-k]))
        if k > 1:
            tb, ta = up(join(tb, pb[k - 1])), down(join(ta, pa[-(k - 1)]))

    def pair(v, axis, n, bits):
        return v + flip(v.astype(BF16), axis, n, bits).astype(F32)

    ranks = pair(ranks_out, "yhi", 2, 1)
    for bits in (1, 2, 4):
        ranks = pair(ranks, "z", ZN, bits)
    ranks = ranks.astype(BF16)
    ranks = ordered(core, ranks, swap(ranks), 1)
    in_grads = SCALE * jnp.concatenate([dot_nn(ranks[0 : 2 * RANK], x), dot_nn(ranks[2 * RANK : RANKS], dy)], axis=0)
    out_grads = grads[:, 0:HID] + swap(grads[:, HID:WIDE])
    sums = jnp.concatenate([in_grads, out_grads], axis=1)
    for axis, n, bits in (("x", 4, 1), ("x", 4, 2), ("ylo", 2, 1)):
        sums = sums + flip(sums, axis, n, bits)

    total_a = pa[0] + sa.astype(F32) + ta.astype(F32)
    total_b = pb[0] + sb.astype(F32) + tb.astype(F32)
    total = (total_a + flip(total_b.astype(BF16), "yhi", 2, 1).astype(F32)).astype(BF16)
    low, high = total[:, 0:LANES], total[:, LANES:FEATS]
    first = core == 0
    got = swap(jnp.where(first, high, low))
    rows_grad = ordered(core, jnp.where(first, low, high), got, 0)
    g = [sums[i * RANK : (i + 1) * RANK, 0:LANES] for i in range(3)]
    o = [sums[i * RANK : (i + 1) * RANK, LANES:] for i in range(3)]
    return rows_grad, g[0], o[0], g[1], o[1], o[2], g[2]


def solution(mesh):
    split = Mesh(mesh.devices.reshape(2, 4, 2, 8, 2), ("ylo", "x", "yhi", "z", "core"))
    dp, tensor = ("ylo", "x"), ("yhi", "z", "core")
    cols = P(None, tensor)
    return jax.shard_map(
        body,
        mesh=split,
        in_specs=(P(dp, tensor), P(dp, tensor), cols, cols, P(tensor, None), cols, cols, cols, cols, cols, cols),
        out_specs=(P(dp, tensor), cols, cols, cols, cols, cols, cols),
        check_vma=False,
    )
```

```python
import functools

import jax
import jax.numpy as jnp
from jax import lax
from jax.experimental import pallas as pl
from jax.experimental.pallas import tpu as pltpu
from jax.sharding import Mesh, PartitionSpec as P

SCALE = 0.5
ROWS = 512
HALF = ROWS // 2
LANES = 128
FEATS = 2 * LANES
HID = 512
RANK = 32
RANKS = 3 * RANK
PIECE = 2 * ROWS + RANKS
ZN = 8
VMEM_LIMIT = 16 * 1024 * 1024
F32 = jnp.float32
BF16 = jnp.bfloat16

VM = pl.BlockSpec(memory_space=pltpu.VMEM)
SM = pl.BlockSpec(memory_space=pltpu.SMEM)
OWN, OTHER = 0, 1


def dot_nn(a, b):
    return lax.dot_general(a, b, (((1,), (0,)), ((), ())), preferred_element_type=F32)


def dot_nt(a, b):
    return lax.dot_general(a, b, (((1,), (1,)), ((), ())), preferred_element_type=F32)


def dot_tn(a, b):
    return lax.dot_general(a, b, (((0,), (0,)), ((), ())), preferred_element_type=F32)


def feature_at(idx, block):
    k, r = block
    core = idx[2]
    r = {"near": core, "far": 1 - core}.get(r, r)
    yhi = lax.rem(idx[0] + r, 2)
    z = lax.rem(idx[1] + k * (1 - 2 * core) + ZN, ZN)
    return pl.multiple_of((yhi * ZN + z) * FEATS, FEATS)


def params():
    return pltpu.CompilerParams(vmem_limit_bytes=VMEM_LIMIT)


def keep(v):
    return pltpu.with_memory_space_constraint(v, pltpu.VMEM)


def stay(v):
    return pltpu.with_memory_space_constraint(v, pltpu.HBM)


def shape(rows, cols, dtype):
    return jax.ShapeDtypeStruct((rows, cols), dtype)


def pack_kernel(x, dy, gif, uif, dof, out, sem):
    at, copies = 0, []
    for i, ref in enumerate((x, dy, gif, uif, dof)):
        rows = ref.shape[0]
        copies.append(pltpu.make_async_copy(ref, out.at[at : at + rows, :], sem.at[i]))
        at += rows
    for c in copies:
        c.start()
    for c in copies:
        c.wait()


def pack(*arrays):
    return pl.pallas_call(
        pack_kernel,
        out_shape=shape(PIECE, LANES, BF16),
        in_specs=[pl.BlockSpec(memory_space=pl.ANY)] * 5,
        out_specs=VM,
        scratch_shapes=[pltpu.SemaphoreType.DMA((5,))],
        compiler_params=params(),
    )(*map(stay, arrays))


def ordered_kernel(idx, mine, theirs, out):
    @pl.when(idx[2] == 0)
    def _():
        out[:, 0:LANES] = mine[...]
        out[:, LANES:FEATS] = theirs[...]

    @pl.when(idx[2] != 0)
    def _():
        out[:, 0:LANES] = theirs[...]
        out[:, LANES:FEATS] = mine[...]


def ordered(idx, mine, theirs):
    return pl.pallas_call(
        ordered_kernel,
        out_shape=shape(PIECE, FEATS, BF16),
        in_specs=[SM, VM, VM],
        out_specs=VM,
        compiler_params=params(),
    )(idx, mine, theirs)


def accumulate(blocks, first, idx, pieces, weights, accs, outs):
    wg, wu, wd = weights
    at = [feature_at(idx, b) for b in blocks]
    x, c, f = (
        jnp.concatenate([p[lo:hi, :] for p in pieces], axis=1)
        for lo, hi in ((0, ROWS), (ROWS, 2 * ROWS), (2 * ROWS, PIECE))
    )

    def put(i, sl, val):
        outs[i][sl] = val if first else accs[i][sl] + val

    put(0, Ellipsis, dot_nn(x, jnp.concatenate([wg[pl.ds(a, FEATS), :] for a in at], axis=0)))
    put(1, Ellipsis, dot_nn(x, jnp.concatenate([wu[pl.ds(a, FEATS), :] for a in at], axis=0)))
    put(2, Ellipsis, dot_nt(c, jnp.concatenate([wd[:, pl.ds(a, FEATS)] for a in at], axis=1)))
    put(3, (slice(0, 2 * RANK), slice(None)), dot_nt(f[0 : 2 * RANK], x))
    put(3, (slice(2 * RANK, RANKS), slice(None)), dot_nt(f[2 * RANK : RANKS], c))


def acc_kernel(blocks, first, idx, p0, p1, wg, wu, wd, *refs):
    accs, outs = (None, refs) if first else (refs[:4], refs[4:])
    accumulate(blocks, first, idx, (p0, p1), (wg, wu, wd), accs, outs)


ACC_SHAPES = [shape(ROWS, HID, F32)] * 3 + [shape(RANKS, ROWS, F32)]


def run_acc(blocks, idx, pieces, weights, accs):
    first = accs is None
    args = [idx, *pieces, *map(keep, weights)] + ([] if first else list(accs))
    aliases = {} if first else {len(args) - 4 + i: i for i in range(4)}
    return pl.pallas_call(
        functools.partial(acc_kernel, blocks, first),
        out_shape=ACC_SHAPES,
        in_specs=[SM] + [VM] * (len(args) - 1),
        out_specs=[VM] * 4,
        input_output_aliases=aliases,
        compiler_params=params(),
        cost_estimate=pl.CostEstimate(flops=2 * ROWS * HID * HID * 4, bytes_accessed=2**20, transcendentals=0),
    )(*args)


def mid_kernel(blocks, idx, p0, p1, wg, wu, wd, *refs):
    accs, (gof, uof, dif), (out, ranks_out, grads), (g, u, h, rt, hid) = refs[:4], refs[4:7], refs[7:10], refs[10:15]
    accumulate(blocks, False, idx, (p0, p1), (wg, wu, wd), accs, (g, u, h, rt))
    ranks = rt[...].astype(BF16)
    for i, (ref, fac) in enumerate(((g, gof), (u, uof), (h, dif))):
        ref[...] += SCALE * dot_tn(ranks[i * RANK : (i + 1) * RANK], fac[...])
    step = 64

    @pl.loop(0, ROWS // step)
    def _(i):
        at = pl.ds(pl.multiple_of(i * step, step), step)
        gate, up, grad = g[at, :], u[at, :], h[at, :]
        sig = jax.nn.sigmoid(gate)
        act = gate * sig
        hid[at, :] = (act * up).astype(BF16)
        out[at, 0:HID] = (grad * up * sig * (1.0 + gate * (1.0 - sig))).astype(BF16)
        out[at, HID : 2 * HID] = (grad * act).astype(BF16)

    three = (out[0:ROWS, 0:HID], out[0:ROWS, HID : 2 * HID], hid[...])
    for i, (val, fac) in enumerate(zip(three, (gof, uof, dif))):
        at = slice(i * RANK, (i + 1) * RANK)
        ranks_out[at, :] = dot_nt(fac[...], val)
        grads[at, :] = SCALE * dot_nn(ranks[at], val)
    out[ROWS : ROWS + RANKS, 0:HID] = ranks_out[...].astype(BF16)
    out[ROWS : ROWS + RANKS, HID : 2 * HID] = jnp.zeros((RANKS, HID), BF16)


def run_mid(blocks, idx, pieces, weights, accs, factors):
    args = [idx, *pieces, *map(keep, weights), *accs, *factors]
    return pl.pallas_call(
        functools.partial(mid_kernel, blocks),
        out_shape=[shape(ROWS + RANKS, 2 * HID, BF16), shape(RANKS, ROWS, F32), shape(RANKS, HID, F32)],
        in_specs=[SM] + [VM] * (len(args) - 1),
        out_specs=[VM] * 3,
        scratch_shapes=[
            pltpu.VMEM((ROWS, HID), F32),
            pltpu.VMEM((ROWS, HID), F32),
            pltpu.VMEM((ROWS, HID), F32),
            pltpu.VMEM((RANKS, ROWS), F32),
            pltpu.VMEM((ROWS, HID), BF16),
        ],
        compiler_params=params(),
        cost_estimate=pl.CostEstimate(
            flops=2 * ROWS * HID * HID * 6, bytes_accessed=2**20, transcendentals=ROWS * HID
        ),
    )(*args)


def out_kernel(blocks, parts, added, idx, *refs):
    refs = list(refs)
    wides, refs = refs[:parts], refs[parts:]
    weights, refs = refs[: 2 * parts], refs[2 * parts :]
    before = None
    if added:
        before, refs = refs[: len(blocks)], refs[len(blocks) :]
    outs = refs
    for s, b in enumerate(blocks):
        at = pl.ds(feature_at(idx, b), FEATS)
        total = before[s][...] if added else None
        for p in range(parts):
            for i in range(2):
                term = dot_nt(wides[p][0:ROWS, i * HID : (i + 1) * HID], weights[2 * p + i][at, :])
                total = term if total is None else total + term
        outs[s][...] = total.astype(outs[s].dtype)


def run_out(blocks, idx, wides, weights, before, dtype):
    added = before is not None
    args = [idx, *wides, *map(keep, weights)] + (list(before) if added else [])
    return pl.pallas_call(
        functools.partial(out_kernel, blocks, len(wides), added),
        out_shape=[shape(ROWS, FEATS, dtype)] * len(blocks),
        in_specs=[SM] + [VM] * (len(args) - 1),
        out_specs=[VM] * len(blocks),
        compiler_params=params(),
        cost_estimate=pl.CostEstimate(
            flops=len(blocks) * len(wides) * 2 * ROWS * FEATS * 2 * HID, bytes_accessed=2**20, transcendentals=0
        ),
    )(*args)


def flip(v, axis, n, bits):
    return lax.ppermute(v, axis, [(i, i ^ bits) for i in range(n)])


def swap(v):
    return flip(v, "core", 2, 1)


def along(v):
    return lax.ppermute(v, ("z", "core"), [(2 * z + c, 2 * ((z + 1 - 2 * c) % ZN) + c) for z in range(ZN) for c in (0, 1)])


def after(v, done):
    return lax.optimization_barrier((v, done))[0]


def body(x, dy, wg, wu, wd, gif, gof, uif, uof, dif, dof):
    yhi, z, core = lax.axis_index("yhi"), lax.axis_index("z"), lax.axis_index("core")
    idx = jnp.stack([yhi, z, core]).astype(jnp.int32)
    first = core == 0

    own = pack(x, dy, gif, uif, dof)
    a0 = ordered(idx, own, swap(own))
    other = after(flip(own, "yhi", 2, 1), a0)
    a1 = along(a0)
    b0 = ordered(idx, other, swap(other))
    b1 = along(b0)
    their_wg = swap(after(wg, b0))
    their_wu = swap(after(wu, their_wg))
    weights = (wg, wu, wd)

    accs = run_acc(((0, 0), (0, 1)), idx, (a0, b0), weights, None)
    a2 = along(a1)
    b2 = along(b1)
    accs_a1 = run_acc(((-1, 0), (1, 0)), idx, (a1, swap(a1)), weights, accs)
    a3 = along(after(a2, accs_a1[3]))
    accs_b1 = run_acc(((-1, 1), (1, 1)), idx, (b1, swap(b1)), weights, accs_a1)
    b3 = along(after(b2, accs_b1[3]))
    accs = run_acc(((-2, 0), (2, 0)), idx, (a2, swap(a2)), weights, accs_b1)
    last = along(after(jnp.where(first, a3, b3), accs[3]))
    accs = run_acc(((-2, 1), (2, 1)), idx, (b2, swap(b2)), weights, accs)
    accs = run_acc(((-3, 0), (3, 0)), idx, (a3, swap(a3)), weights, accs)
    accs = run_acc(((-3, 1), (3, 1)), idx, (b3, swap(b3)), weights, accs)
    wide, ranks_out, grads = run_mid(
        ((4, "near"), (4, "far")), idx, (last, swap(last)), weights, accs, (gof, uof, dif)
    )
    their = swap(wide)
    mine_w, their_w = (wg, wu), (their_wg, their_wu)

    k1 = ((4, "near"), (3, "far"))
    k2 = ((3, "near"), (2, "far"))
    k3 = ((2, "near"), (1, "far"))
    k4 = ((1, "near"), (0, "near"))
    part = run_out(k1 + k2, idx, (wide,), mine_w, None, F32)
    n4, f3 = run_out(k1, idx, (their,), their_w, part[0:2], BF16)
    near, far = along(n4), along(f3)
    n3, f2 = run_out(k2, idx, (after(their, n4),), their_w, part[2:4], F32)
    n2, f1 = run_out(k3, idx, (wide, their), mine_w + their_w, None, F32)
    n1, n0 = run_out(k4, idx, (wide, their), mine_w + their_w, None, F32)

    def join(moving, here):
        return (moving.astype(F32) + here).astype(BF16)

    def pair(v, axis, n, bits, done):
        return v + flip(after(v.astype(BF16), done), axis, n, bits).astype(F32)

    both = ranks_out + their[ROWS : ROWS + RANKS, 0:HID].astype(F32)
    ranks = lax.dynamic_slice_in_dim(both, core * HALF, HALF, axis=1)
    ranks = pair(ranks, "yhi", 2, 1, n4)
    near_2 = join(near, n3)
    near = along(near_2)
    ranks = pair(ranks, "z", ZN, 1, near_2)
    far_2 = join(far, f2)
    far = along(far_2)
    ranks = pair(ranks, "z", ZN, 2, far_2)
    near_3 = join(near, n2)
    near = along(near_3)
    ranks = pair(ranks, "z", ZN, 4, near_3).astype(BF16)
    far_3 = join(far, f1)
    far = along(far_3)
    other_ranks = swap(after(ranks, far_3))
    ranks = jnp.where(
        first, jnp.concatenate([ranks, other_ranks], axis=1), jnp.concatenate([other_ranks, ranks], axis=1)
    )
    in_grads = SCALE * jnp.concatenate([dot_nn(ranks[0 : 2 * RANK], x), dot_nn(ranks[2 * RANK : RANKS], dy)], axis=0)
    near_4 = join(near, n1)
    near = along(near_4)
    sums = after(jnp.concatenate([in_grads, grads], axis=1), near_4)
    for axis, n, bits in (("x", 4, 1), ("x", 4, 2), ("ylo", 2, 1)):
        sums = sums + flip(sums, axis, n, bits)
    adapter = SCALE * dot_tn(ranks[0 : 2 * RANK], jnp.concatenate([gif, uif], axis=0))

    total = n0 + near.astype(F32) + swap(far).astype(F32)
    low, high = total[:, 0:LANES], total[:, LANES:FEATS]
    cross = [(0, 1), (1, 2), (2, 3), (3, 0)]
    got = lax.ppermute(jnp.where(first, high, low).astype(BF16), ("yhi", "core"), cross)
    more = lax.ppermute(high.astype(BF16), ("yhi", "core"), [(1, 3), (3, 1), (0, 0), (2, 2)])
    rows_grad = got.astype(F32) + jnp.where(first, low, more.astype(F32)) + adapter
    g = [sums[i * RANK : (i + 1) * RANK, 0:LANES] for i in range(3)]
    o = [sums[i * RANK : (i + 1) * RANK, LANES:] for i in range(3)]
    return rows_grad.astype(BF16), g[0], o[0], g[1], o[1], o[2], g[2]


def solution(mesh):
    split = Mesh(mesh.devices.reshape(2, 4, 2, 8, 2), ("ylo", "x", "yhi", "z", "core"))
    dp, tensor = ("ylo", "x"), ("yhi", "z", "core")
    cols = P(None, tensor)
    return jax.shard_map(
        body,
        mesh=split,
        in_specs=(P(dp, tensor), P(dp, tensor), cols, cols, P(tensor, None), cols, cols, cols, cols, cols, cols),
        out_specs=(P(dp, tensor), cols, cols, cols, cols, cols, cols),
        check_vma=False,
    )
```

```python
import functools

import jax
import jax.numpy as jnp
from jax import lax
from jax.experimental import pallas as pl
from jax.experimental.pallas import tpu as pltpu
from jax.sharding import Mesh, PartitionSpec as P

SCALE = 0.5
ROWS = 512
HALF = ROWS // 2
LANES = 128
FEATS = 2 * LANES
HID = 512
RANK = 32
RANKS = 3 * RANK
PIECE = 2 * ROWS + RANKS
PART = PIECE // 2
ZN = 8
VMEM_LIMIT = 16 * 1024 * 1024
F32 = jnp.float32
BF16 = jnp.bfloat16

VM = pl.BlockSpec(memory_space=pltpu.VMEM)
SM = pl.BlockSpec(memory_space=pltpu.SMEM)
COST = pl.CostEstimate(flops=1, bytes_accessed=1, transcendentals=0)
ACC_COST = COST
PART_COST = pl.CostEstimate(flops=8 * 10**9, bytes_accessed=1, transcendentals=0)


def dot_nn(a, b):
    return lax.dot_general(a, b, (((1,), (0,)), ((), ())), preferred_element_type=F32)


def dot_nt(a, b):
    return lax.dot_general(a, b, (((1,), (1,)), ((), ())), preferred_element_type=F32)


def dot_tn(a, b):
    return lax.dot_general(a, b, (((0,), (0,)), ((), ())), preferred_element_type=F32)


def feature_at(idx, block):
    k, r = block
    core = idx[2]
    r = {"near": core, "far": 1 - core}.get(r, r)
    yhi = lax.rem(idx[0] + r, 2)
    z = lax.rem(idx[1] + k * (1 - 2 * core) + ZN, ZN)
    return pl.multiple_of((yhi * ZN + z) * FEATS, FEATS)


def params():
    return pltpu.CompilerParams(vmem_limit_bytes=VMEM_LIMIT)


def keep(v):
    return pltpu.with_memory_space_constraint(v, pltpu.VMEM)


def stay(v):
    return pltpu.with_memory_space_constraint(v, pltpu.HBM)


def shape(rows, cols, dtype):
    return jax.ShapeDtypeStruct((rows, cols), dtype)


def pack_kernel(x, dy, gif, uif, dof, out, sem):
    at, copies = 0, []
    for i, ref in enumerate((x, dy, gif, uif, dof)):
        rows = ref.shape[0]
        copies.append(pltpu.make_async_copy(ref, out.at[at : at + rows, :], sem.at[i]))
        at += rows
    for c in copies:
        c.start()
    for c in copies:
        c.wait()


def pack(*arrays):
    return pl.pallas_call(
        pack_kernel,
        out_shape=shape(PIECE, LANES, BF16),
        in_specs=[pl.BlockSpec(memory_space=pl.ANY)] * 5,
        out_specs=VM,
        scratch_shapes=[pltpu.SemaphoreType.DMA((5,))],
        compiler_params=params(),
        cost_estimate=COST,
    )(*map(stay, arrays))


def load_kernel(*refs):
    n = len(refs) // 2
    ins, outs, sem = refs[:n], refs[n : 2 * n], refs[2 * n]
    copies = [pltpu.make_async_copy(a, b, sem.at[i]) for i, (a, b) in enumerate(zip(ins, outs))]
    for c in copies:
        c.start()
    for c in copies:
        c.wait()


def load(*arrays):
    return pl.pallas_call(
        load_kernel,
        out_shape=[jax.ShapeDtypeStruct(a.shape, a.dtype) for a in arrays],
        in_specs=[pl.BlockSpec(memory_space=pl.ANY)] * len(arrays),
        out_specs=[VM] * len(arrays),
        scratch_shapes=[pltpu.SemaphoreType.DMA((len(arrays),))],
        compiler_params=params(),
        cost_estimate=COST,
    )(*map(stay, arrays))


BLOCKS = ((4, "near"), (3, "far"), (3, "near"), (2, "far"), (2, "near"), (1, "far"), (1, "near"), (0, "near"))


def choose_kernel(idx, wg, wu, out, sem):
    other = (idx[0], idx[1], 1 - idx[2])
    copies = []
    for s, b in enumerate(BLOCKS):
        at = pl.ds(feature_at(other, b), FEATS)
        for i, w in enumerate((wg, wu)):
            to = out.at[pl.ds((2 * s + i) * FEATS, FEATS), :]
            copies.append(pltpu.make_async_copy(w.at[at, :], to, sem.at[s, i]))
    for c in copies:
        c.start()
    for c in copies:
        c.wait()


def choose(idx, wg, wu):
    return pl.pallas_call(
        choose_kernel,
        out_shape=shape(2 * len(BLOCKS) * FEATS, HID, BF16),
        in_specs=[SM] + [pl.BlockSpec(memory_space=pl.ANY)] * 2,
        out_specs=VM,
        scratch_shapes=[pltpu.SemaphoreType.DMA((len(BLOCKS), 2))],
        compiler_params=params(),
        cost_estimate=COST,
    )(idx, stay(wg), stay(wu))


def ordered_kernel(idx, mine, theirs, out):
    @pl.when(idx[2] == 0)
    def _():
        out[:, 0:LANES] = mine[...]
        out[:, LANES:FEATS] = theirs[...]

    @pl.when(idx[2] != 0)
    def _():
        out[:, 0:LANES] = theirs[...]
        out[:, LANES:FEATS] = mine[...]


def ordered(idx, mine, theirs):
    return pl.pallas_call(
        ordered_kernel,
        out_shape=shape(PIECE, FEATS, BF16),
        in_specs=[SM, VM, VM],
        out_specs=VM,
        compiler_params=params(),
        cost_estimate=COST,
    )(idx, mine, theirs)


def accumulate(blocks, first, idx, pieces, weights, accs, outs):
    wg, wu, wd = weights
    at = [feature_at(idx, b) for b in blocks]
    x, c, f = (
        jnp.concatenate([p[lo:hi, :] for p in pieces], axis=1)
        for lo, hi in ((0, ROWS), (ROWS, 2 * ROWS), (2 * ROWS, PIECE))
    )

    def put(i, sl, val):
        outs[i][sl] = val if first else accs[i][sl] + val

    put(0, Ellipsis, dot_nn(x, jnp.concatenate([wg[pl.ds(a, FEATS), :] for a in at], axis=0)))
    put(1, Ellipsis, dot_nn(x, jnp.concatenate([wu[pl.ds(a, FEATS), :] for a in at], axis=0)))
    put(2, Ellipsis, dot_nt(c, jnp.concatenate([wd[:, pl.ds(a, FEATS)] for a in at], axis=1)))
    put(3, (slice(0, 2 * RANK), slice(None)), dot_nt(f[0 : 2 * RANK], x))
    put(3, (slice(2 * RANK, RANKS), slice(None)), dot_nt(f[2 * RANK : RANKS], c))


def acc_kernel(blocks, first, idx, p0, p1, wg, wu, wd, *refs):
    accs, outs = (None, refs) if first else (refs[:4], refs[4:])
    accumulate(blocks, first, idx, (p0, p1), (wg, wu, wd), accs, outs)


ACC_SHAPES = [shape(ROWS, HID, F32)] * 3 + [shape(RANKS, ROWS, F32)]


def run_acc(blocks, idx, pieces, weights, accs):
    first = accs is None
    args = [idx, *pieces, *map(keep, weights)] + ([] if first else list(accs))
    aliases = {} if first else {len(args) - 4 + i: i for i in range(4)}
    return pl.pallas_call(
        functools.partial(acc_kernel, blocks, first),
        out_shape=ACC_SHAPES,
        in_specs=[SM] + [VM] * (len(args) - 1),
        out_specs=[VM] * 4,
        input_output_aliases=aliases,
        compiler_params=params(),
        cost_estimate=ACC_COST,
    )(*args)


def joined(idx, mine, theirs, whole):
    at = pl.multiple_of(idx[2] * PART, PART)
    whole[pl.ds(at, PART), :] = mine[...]
    whole[pl.ds(PART - at, PART), :] = theirs[...]
    return whole


def part_kernel(block, idx, mine, theirs, wg, wu, wd, *refs):
    accs, outs, whole = refs[:4], refs[4:8], refs[8]
    accumulate((block,), False, idx, (joined(idx, mine, theirs, whole),), (wg, wu, wd), accs, outs)


def run_part(block, idx, pieces, weights, accs):
    args = [idx, *pieces, *map(keep, weights), *accs]
    return pl.pallas_call(
        functools.partial(part_kernel, block),
        out_shape=ACC_SHAPES,
        in_specs=[SM] + [VM] * (len(args) - 1),
        out_specs=[VM] * 4,
        scratch_shapes=[pltpu.VMEM((PIECE, FEATS), BF16)],
        input_output_aliases={len(args) - 4 + i: i for i in range(4)},
        compiler_params=params(),
        cost_estimate=PART_COST,
    )(*args)


def half_kernel(idx, piece, out):
    out[...] = piece[pl.ds(pl.multiple_of(idx[2] * PART, PART), PART), :]


def half_of(idx, piece):
    return pl.pallas_call(
        half_kernel,
        out_shape=shape(PART, FEATS, BF16),
        in_specs=[SM, VM],
        out_specs=VM,
        compiler_params=params(),
        cost_estimate=COST,
    )(idx, piece)


def mid_kernel(block, idx, mine, theirs, wg, wu, wd, *refs):
    accs, (gof, uof, dif), (out, sent, ranks_out, grads), (g, u, h, rt, hid, whole) = (
        refs[:4],
        refs[4:7],
        refs[7:11],
        refs[11:17],
    )
    accumulate((block,), False, idx, (joined(idx, mine, theirs, whole),), (wg, wu, wd), accs, (g, u, h, rt))
    ranks = rt[...].astype(BF16)
    for i, (ref, fac) in enumerate(((g, gof), (u, uof), (h, dif))):
        ref[...] += SCALE * dot_tn(ranks[i * RANK : (i + 1) * RANK], fac[...])
    step = 64

    @pl.loop(0, ROWS // step)
    def _(i):
        at = pl.ds(pl.multiple_of(i * step, step), step)
        gate, up, grad = g[at, :], u[at, :], h[at, :]
        sig = jax.nn.sigmoid(gate)
        act = gate * sig
        hid[at, :] = (act * up).astype(BF16)
        gate_grad = (grad * up * sig * (1.0 + gate * (1.0 - sig))).astype(BF16)
        up_grad = (grad * act).astype(BF16)
        for ref in (out, sent):
            ref[at, 0:HID] = gate_grad
            ref[at, HID : 2 * HID] = up_grad

    three = (out[0:ROWS, 0:HID], out[0:ROWS, HID : 2 * HID], hid[...])
    for i, (val, fac) in enumerate(zip(three, (gof, uof, dif))):
        at = slice(i * RANK, (i + 1) * RANK)
        ranks_out[at, :] = dot_nt(fac[...], val)
        grads[at, :] = SCALE * dot_nn(ranks[at], val)
    sent[ROWS : ROWS + RANKS, 0:HID] = ranks_out[...].astype(BF16)
    sent[ROWS : ROWS + RANKS, HID : 2 * HID] = jnp.zeros((RANKS, HID), BF16)


def run_mid(block, idx, pieces, weights, accs, factors):
    args = [idx, *pieces, *map(keep, weights), *accs, *factors]
    return pl.pallas_call(
        functools.partial(mid_kernel, block),
        out_shape=[
            shape(ROWS, 2 * HID, BF16),
            shape(ROWS + RANKS, 2 * HID, BF16),
            shape(RANKS, ROWS, F32),
            shape(RANKS, HID, F32),
        ],
        in_specs=[SM] + [VM] * (len(args) - 1),
        out_specs=[VM] * 4,
        scratch_shapes=[
            pltpu.VMEM((ROWS, HID), F32),
            pltpu.VMEM((ROWS, HID), F32),
            pltpu.VMEM((ROWS, HID), F32),
            pltpu.VMEM((RANKS, ROWS), F32),
            pltpu.VMEM((ROWS, HID), BF16),
            pltpu.VMEM((PIECE, FEATS), BF16),
        ],
        compiler_params=params(),
        cost_estimate=COST,
    )(*args)


def out_kernel(blocks, own, other, added, idx, *refs):
    refs = list(refs)
    wides = [refs.pop(0) for _ in range(own + other)]
    mine, theirs = refs[: 2 * own], refs[2 * own : 2 * own + other]
    refs = refs[2 * own + other :]
    before, outs = refs[: len(blocks)], refs[-len(blocks) :]
    for s, b in enumerate(blocks):
        terms = []
        if own:
            at = pl.ds(feature_at(idx, b), FEATS)
            terms += [(wides[0], w[at, :]) for w in mine]
        if other:
            at = 2 * BLOCKS.index(b) * FEATS
            terms += [(wides[-1], theirs[0][at + i * FEATS : at + (i + 1) * FEATS, :]) for i in range(2)]
        total = before[s][...] if added else None
        for i, (wide, w) in enumerate(terms):
            i = i % 2
            term = dot_nt(wide[0:ROWS, i * HID : (i + 1) * HID], w)
            total = term if total is None else total + term
        outs[s][...] = total.astype(outs[s].dtype)


def run_out(blocks, idx, wide, their, own_weights, their_weights, before, dtype):
    own, other, added = wide is not None, their is not None, before is not None
    args = [idx] + [wide] * own + [their] * other
    args += [keep(w) for w in (own_weights or ()) + ((their_weights,) if other else ())] + list(before or ())
    return pl.pallas_call(
        functools.partial(out_kernel, blocks, int(own), int(other), added),
        out_shape=[shape(ROWS, FEATS, dtype)] * len(blocks),
        in_specs=[SM] + [VM] * (len(args) - 1),
        out_specs=[VM] * len(blocks),
        compiler_params=params(),
        cost_estimate=COST,
    )(*args)


def rank_kernel(idx, ranks_out, their, out):
    at = pl.ds(pl.multiple_of(idx[2] * HALF, HALF), HALF)
    out[...] = ranks_out[:, at] + their[ROWS : ROWS + RANKS, at].astype(F32)


def chip_ranks(idx, ranks_out, their):
    return pl.pallas_call(
        rank_kernel,
        out_shape=shape(RANKS, HALF, F32),
        in_specs=[SM, VM, VM],
        out_specs=VM,
        compiler_params=params(),
        cost_estimate=COST,
    )(idx, ranks_out, their)


def join(moving, here):
    return (moving.astype(F32) + here).astype(BF16)


def flip(v, axis, n, bits):
    return lax.ppermute(v, axis, [(i, i ^ bits) for i in range(n)])


def swap(v):
    return flip(v, "core", 2, 1)


def along(v):
    return lax.ppermute(v, ("z", "core"), [(2 * z + c, 2 * ((z + 1 - 2 * c) % ZN) + c) for z in range(ZN) for c in (0, 1)])


def after(v, done):
    return lax.optimization_barrier((v, done))[0]


def body(x, dy, wg, wu, wd, gif, gof, uif, uof, dif, dof):
    yhi, z, core = lax.axis_index("yhi"), lax.axis_index("z"), lax.axis_index("core")
    idx = jnp.stack([yhi, z, core]).astype(jnp.int32)
    first = core == 0

    own = pack(x, dy, gif, uif, dof)
    a0 = ordered(idx, own, swap(own))
    with jax.named_scope("y"):
        other = flip(after(own, a0), "yhi", 2, 1)
    with jax.named_scope("a1"):
        a1 = along(a0)
    with jax.named_scope("weights"):
        chosen = choose(idx, after(wg, a0), after(wu, a0))
        their_w = swap(chosen)
        weights = load(*(after(w, a0) for w in (wg, wu, wd)))
    other = after(other, (a1, chosen, weights))
    with jax.named_scope("swap_b0"):
        b0 = ordered(idx, other, swap(other))
    with jax.named_scope("b1"):
        b1 = along(b0)

    def acc(k, r, piece, accs):
        with jax.named_scope(f"swap_{'ab'[r]}{k}"):
            theirs = swap(piece)
        with jax.named_scope(f"acc_{'ab'[r]}{k}"):
            return run_acc(((-k, r), (k, r)), idx, (piece, theirs), weights, accs)

    with jax.named_scope("acc_0"):
        accs = run_acc(((0, 0), (0, 1)), idx, (a0, b0), weights, None)
    with jax.named_scope("a2"):
        a2 = along(a1)
    with jax.named_scope("b2"):
        b2 = along(after(b1, accs[3]))
    accs = acc(1, 0, a1, accs)
    with jax.named_scope("a3"):
        a3 = along(after(a2, accs[3]))
    accs = acc(1, 1, b1, accs)
    with jax.named_scope("b3"):
        b3 = along(after(b2, accs[3]))
    accs = acc(2, 0, a2, accs)
    with jax.named_scope("a4"):
        a4 = along(half_of(idx, after(a3, accs[3])))
    accs = acc(2, 1, b2, accs)
    with jax.named_scope("b4"):
        b4 = along(half_of(idx, after(b3, accs[3])))
    accs = acc(3, 0, a3, accs)
    accs = acc(3, 1, b3, accs)
    with jax.named_scope("swap_a4"):
        a4 = (a4, swap(after(a4, accs[3])))
    with jax.named_scope("acc_a4"):
        accs = run_part((4, 0), idx, a4, weights, accs)
    with jax.named_scope("swap_b4"):
        b4 = (b4, swap(b4))
    with jax.named_scope("mid"):
        wide, sent, ranks_out, grads = run_mid((4, 1), idx, b4, weights, accs, (gof, uof, dif))
    their = swap(sent)
    mine_w = tuple(weights[0:2])
    k1, k2, k3, k4 = (BLOCKS[i : i + 2] for i in range(0, 8, 2))
    with jax.named_scope("own_part"):
        part = run_out(k1 + k2, idx, wide, None, mine_w, None, None, F32)
    with jax.named_scope("out_1"):
        n4, f3 = run_out(k1, idx, None, their, None, their_w, part[0:2], BF16)
    with jax.named_scope("n1"):
        near = along(n4)
    with jax.named_scope("f1"):
        far = along(f3)
    with jax.named_scope("out_2"):
        n3, f2 = run_out(k2, idx, None, their, None, their_w, part[2:4], F32)
    with jax.named_scope("out_3"):
        n2, f1 = run_out(k3, idx, wide, their, mine_w, their_w, None, F32)
    with jax.named_scope("out_4"):
        n1, n0 = run_out(k4, idx, wide, their, mine_w, their_w, None, F32)

    def pair(name, v, axis, n, bits, done=None):
        sent = v.astype(BF16)
        with jax.named_scope(name):
            return v + flip(sent if done is None else after(sent, done), axis, n, bits).astype(F32)

    def total_rows(name, v, axis, n, bits, done=None):
        with jax.named_scope(name):
            return v + flip(v if done is None else after(v, done), axis, n, bits)

    def hop(name, v):
        with jax.named_scope(name):
            return along(v)

    with jax.named_scope("ranks"):
        ranks = chip_ranks(idx, after(ranks_out, part[0]), their)
    ranks = pair("ranks_y", ranks, "yhi", 2, 1)
    ranks = pair("ranks_1", ranks, "z", ZN, 1, n4)
    near_2, far_2 = join(near, after(n3, f1)), join(far, f2)
    near, far = hop("n2", near_2), hop("f2", far_2)
    ranks = pair("ranks_2", ranks, "z", ZN, 2, (near_2, far_2))
    grads = total_rows("out_x1", grads, "x", 4, 1, near_2)
    near_3, far_3 = join(near, after(n2, n0)), join(far, f1)
    near, far = hop("n3", near_3), hop("f3", far_3)
    ranks = pair("ranks_4", ranks, "z", ZN, 4, (near_3, far_3)).astype(BF16)
    grads = total_rows("out_x2", grads, "x", 4, 2, near_3)
    near_4 = join(near, n1)
    near = hop("n4", near_4)
    with jax.named_scope("ranks_core"):
        other_ranks = swap(after(ranks, near_4))
    grads = total_rows("out_y", grads, "ylo", 2, 1, near_4)
    with jax.named_scope("far_core"):
        far = swap(far)
    ranks = jnp.where(
        first, jnp.concatenate([ranks, other_ranks], axis=1), jnp.concatenate([other_ranks, ranks], axis=1)
    )
    in_grads = SCALE * jnp.concatenate([dot_nn(ranks[0 : 2 * RANK], x), dot_nn(ranks[2 * RANK : RANKS], dy)], axis=0)
    in_grads = total_rows("in_x1", in_grads, "x", 4, 1, grads)
    in_grads = total_rows("in_x2", in_grads, "x", 4, 2, (near, far))
    in_grads = total_rows("in_y", in_grads, "ylo", 2, 1)
    adapter = SCALE * dot_tn(ranks[0 : 2 * RANK], jnp.concatenate([gif, uif], axis=0))

    total = n0 + near.astype(F32) + far.astype(F32)
    low, high = total[:, 0:LANES], total[:, LANES:FEATS]
    cross = [(0, 1), (1, 2), (2, 3), (3, 0)]
    got = lax.ppermute(jnp.where(first, high, low).astype(BF16), ("yhi", "core"), cross)
    more = lax.ppermute(high.astype(BF16), ("yhi", "core"), [(1, 3), (3, 1), (0, 0), (2, 2)])
    rows_grad = got.astype(F32) + jnp.where(first, low, more.astype(F32)) + adapter
    g = [in_grads[i * RANK : (i + 1) * RANK] for i in range(3)]
    o = [grads[i * RANK : (i + 1) * RANK] for i in range(3)]
    return rows_grad.astype(BF16), g[0], o[0], g[1], o[1], o[2], g[2]


def solution(mesh):
    split = Mesh(mesh.devices.reshape(2, 4, 2, 8, 2), ("ylo", "x", "yhi", "z", "core"))
    dp, tensor = ("ylo", "x"), ("yhi", "z", "core")
    cols = P(None, tensor)
    return jax.shard_map(
        body,
        mesh=split,
        in_specs=(P(dp, tensor), P(dp, tensor), cols, cols, P(tensor, None), cols, cols, cols, cols, cols, cols),
        out_specs=(P(dp, tensor), cols, cols, cols, cols, cols, cols),
        check_vma=False,
    )
```

```python
import functools

import jax
import jax.numpy as jnp
from jax import lax
from jax.experimental import pallas as pl
from jax.experimental.pallas import tpu as pltpu
from jax.sharding import Mesh, PartitionSpec as P

SCALE = 0.5
ROWS = 512
HALF = ROWS // 2
LANES = 128
FEATS = 2 * LANES
HID = 512
RANK = 32
RANKS = 3 * RANK
PIECE = 2 * ROWS + RANKS
PART = PIECE // 2
ZN = 8
VMEM_LIMIT = 16 * 1024 * 1024
F32 = jnp.float32
BF16 = jnp.bfloat16

VM = pl.BlockSpec(memory_space=pltpu.VMEM)
SM = pl.BlockSpec(memory_space=pltpu.SMEM)
COST = pl.CostEstimate(flops=1, bytes_accessed=1, transcendentals=0)
ACC_COST = COST
PART_COST = pl.CostEstimate(flops=8 * 10**9, bytes_accessed=1, transcendentals=0)


def dot_nn(a, b):
    return lax.dot_general(a, b, (((1,), (0,)), ((), ())), preferred_element_type=F32)


def dot_nt(a, b):
    return lax.dot_general(a, b, (((1,), (1,)), ((), ())), preferred_element_type=F32)


def dot_tn(a, b):
    return lax.dot_general(a, b, (((0,), (0,)), ((), ())), preferred_element_type=F32)


def feature_at(idx, block):
    k, r = block
    core = idx[2]
    r = {"near": core, "far": 1 - core}.get(r, r)
    yhi = lax.rem(idx[0] + r, 2)
    z = lax.rem(idx[1] + k * (1 - 2 * core) + ZN, ZN)
    return pl.multiple_of((yhi * ZN + z) * FEATS, FEATS)


def params():
    return pltpu.CompilerParams(vmem_limit_bytes=VMEM_LIMIT)


def keep(v):
    return pltpu.with_memory_space_constraint(v, pltpu.VMEM)


def stay(v):
    return pltpu.with_memory_space_constraint(v, pltpu.HBM)


def shape(rows, cols, dtype):
    return jax.ShapeDtypeStruct((rows, cols), dtype)


def pack_kernel(x, dy, gif, uif, dof, out, sem):
    at, copies = 0, []
    for i, ref in enumerate((x, dy, gif, uif, dof)):
        rows = ref.shape[0]
        copies.append(pltpu.make_async_copy(ref, out.at[at : at + rows, :], sem.at[i]))
        at += rows
    for c in copies:
        c.start()
    for c in copies:
        c.wait()


def pack(*arrays):
    return pl.pallas_call(
        pack_kernel,
        out_shape=shape(PIECE, LANES, BF16),
        in_specs=[pl.BlockSpec(memory_space=pl.ANY)] * 5,
        out_specs=VM,
        scratch_shapes=[pltpu.SemaphoreType.DMA((5,))],
        compiler_params=params(),
        cost_estimate=COST,
    )(*map(stay, arrays))


def load_kernel(*refs):
    n = len(refs) // 2
    ins, outs, sem = refs[:n], refs[n : 2 * n], refs[2 * n]
    copies = [pltpu.make_async_copy(a, b, sem.at[i]) for i, (a, b) in enumerate(zip(ins, outs))]
    for c in copies:
        c.start()
    for c in copies:
        c.wait()


def load(*arrays):
    return pl.pallas_call(
        load_kernel,
        out_shape=[jax.ShapeDtypeStruct(a.shape, a.dtype) for a in arrays],
        in_specs=[pl.BlockSpec(memory_space=pl.ANY)] * len(arrays),
        out_specs=[VM] * len(arrays),
        scratch_shapes=[pltpu.SemaphoreType.DMA((len(arrays),))],
        compiler_params=params(),
        cost_estimate=COST,
    )(*map(stay, arrays))


BLOCKS = ((4, "near"), (3, "far"), (3, "near"), (2, "far"), (2, "near"), (1, "far"), (1, "near"), (0, "near"))


def choose_kernel(idx, wg, wu, out, sem):
    other = (idx[0], idx[1], 1 - idx[2])
    copies = []
    for s, b in enumerate(BLOCKS):
        at = pl.ds(feature_at(other, b), FEATS)
        for i, w in enumerate((wg, wu)):
            to = out.at[pl.ds((2 * s + i) * FEATS, FEATS), :]
            copies.append(pltpu.make_async_copy(w.at[at, :], to, sem.at[s, i]))
    for c in copies:
        c.start()
    for c in copies:
        c.wait()


def choose(idx, wg, wu):
    return pl.pallas_call(
        choose_kernel,
        out_shape=shape(2 * len(BLOCKS) * FEATS, HID, BF16),
        in_specs=[SM] + [pl.BlockSpec(memory_space=pl.ANY)] * 2,
        out_specs=VM,
        scratch_shapes=[pltpu.SemaphoreType.DMA((len(BLOCKS), 2))],
        compiler_params=params(),
        cost_estimate=COST,
    )(idx, stay(wg), stay(wu))


def ordered_kernel(idx, mine, theirs, out):
    @pl.when(idx[2] == 0)
    def _():
        out[:, 0:LANES] = mine[...]
        out[:, LANES:FEATS] = theirs[...]

    @pl.when(idx[2] != 0)
    def _():
        out[:, 0:LANES] = theirs[...]
        out[:, LANES:FEATS] = mine[...]


def ordered(idx, mine, theirs):
    return pl.pallas_call(
        ordered_kernel,
        out_shape=shape(PIECE, FEATS, BF16),
        in_specs=[SM, VM, VM],
        out_specs=VM,
        compiler_params=params(),
        cost_estimate=COST,
    )(idx, mine, theirs)


def accumulate(blocks, first, idx, pieces, weights, accs, outs):
    wg, wu, wd = weights
    at = [feature_at(idx, b) for b in blocks]
    x, c, f = (
        jnp.concatenate([p[lo:hi, :] for p in pieces], axis=1)
        for lo, hi in ((0, ROWS), (ROWS, 2 * ROWS), (2 * ROWS, PIECE))
    )

    def put(i, sl, val):
        outs[i][sl] = val if first else accs[i][sl] + val

    put(0, Ellipsis, dot_nn(x, jnp.concatenate([wg[pl.ds(a, FEATS), :] for a in at], axis=0)))
    put(1, Ellipsis, dot_nn(x, jnp.concatenate([wu[pl.ds(a, FEATS), :] for a in at], axis=0)))
    put(2, Ellipsis, dot_nt(c, jnp.concatenate([wd[:, pl.ds(a, FEATS)] for a in at], axis=1)))
    put(3, (slice(0, 2 * RANK), slice(None)), dot_nt(f[0 : 2 * RANK], x))
    put(3, (slice(2 * RANK, RANKS), slice(None)), dot_nt(f[2 * RANK : RANKS], c))


def acc_kernel(blocks, first, idx, p0, p1, wg, wu, wd, *refs):
    accs, outs = (None, refs) if first else (refs[:4], refs[4:])
    accumulate(blocks, first, idx, (p0, p1), (wg, wu, wd), accs, outs)


ACC_SHAPES = [shape(ROWS, HID, F32)] * 3 + [shape(RANKS, ROWS, F32)]


def run_acc(blocks, idx, pieces, weights, accs):
    first = accs is None
    args = [idx, *pieces, *map(keep, weights)] + ([] if first else list(accs))
    aliases = {} if first else {len(args) - 4 + i: i for i in range(4)}
    return pl.pallas_call(
        functools.partial(acc_kernel, blocks, first),
        out_shape=ACC_SHAPES,
        in_specs=[SM] + [VM] * (len(args) - 1),
        out_specs=[VM] * 4,
        input_output_aliases=aliases,
        compiler_params=params(),
        cost_estimate=ACC_COST,
    )(*args)


def joined(idx, mine, theirs, whole):
    at = pl.multiple_of(idx[2] * PART, PART)
    whole[pl.ds(at, PART), :] = mine[...]
    whole[pl.ds(PART - at, PART), :] = theirs[...]
    return whole


def part_kernel(block, idx, mine, theirs, wg, wu, wd, *refs):
    accs, outs, whole = refs[:4], refs[4:8], refs[8]
    accumulate((block,), False, idx, (joined(idx, mine, theirs, whole),), (wg, wu, wd), accs, outs)


def run_part(block, idx, pieces, weights, accs):
    args = [idx, *pieces, *map(keep, weights), *accs]
    return pl.pallas_call(
        functools.partial(part_kernel, block),
        out_shape=ACC_SHAPES,
        in_specs=[SM] + [VM] * (len(args) - 1),
        out_specs=[VM] * 4,
        scratch_shapes=[pltpu.VMEM((PIECE, FEATS), BF16)],
        input_output_aliases={len(args) - 4 + i: i for i in range(4)},
        compiler_params=params(),
        cost_estimate=PART_COST,
    )(*args)


def half_kernel(idx, piece, out):
    out[...] = piece[pl.ds(pl.multiple_of(idx[2] * PART, PART), PART), :]


def half_of(idx, piece):
    return pl.pallas_call(
        half_kernel,
        out_shape=shape(PART, FEATS, BF16),
        in_specs=[SM, VM],
        out_specs=VM,
        compiler_params=params(),
        cost_estimate=COST,
    )(idx, piece)


def mid_kernel(block, idx, mine, theirs, wg, wu, wd, *refs):
    accs, (gof, uof, dif), (out, sent, ranks_out, grads), (g, u, h, rt, hid, whole) = (
        refs[:4],
        refs[4:7],
        refs[7:11],
        refs[11:17],
    )
    accumulate((block,), False, idx, (joined(idx, mine, theirs, whole),), (wg, wu, wd), accs, (g, u, h, rt))
    ranks = rt[...].astype(BF16)
    for i, (ref, fac) in enumerate(((g, gof), (u, uof), (h, dif))):
        ref[...] += SCALE * dot_tn(ranks[i * RANK : (i + 1) * RANK], fac[...])
    step = 64

    @pl.loop(0, ROWS // step)
    def _(i):
        at = pl.ds(pl.multiple_of(i * step, step), step)
        gate, up, grad = g[at, :], u[at, :], h[at, :]
        sig = jax.nn.sigmoid(gate)
        act = gate * sig
        hid[at, :] = (act * up).astype(BF16)
        gate_grad = (grad * up * sig * (1.0 + gate * (1.0 - sig))).astype(BF16)
        up_grad = (grad * act).astype(BF16)
        for ref in (out, sent):
            ref[at, 0:HID] = gate_grad
            ref[at, HID : 2 * HID] = up_grad

    three = (out[0:ROWS, 0:HID], out[0:ROWS, HID : 2 * HID], hid[...])
    for i, (val, fac) in enumerate(zip(three, (gof, uof, dif))):
        at = slice(i * RANK, (i + 1) * RANK)
        ranks_out[at, :] = dot_nt(fac[...], val)
        grads[at, :] = SCALE * dot_nn(ranks[at], val)
    sent[ROWS : ROWS + RANKS, 0:HID] = ranks_out[...].astype(BF16)
    sent[ROWS : ROWS + RANKS, HID : 2 * HID] = jnp.zeros((RANKS, HID), BF16)


def run_mid(block, idx, pieces, weights, accs, factors):
    args = [idx, *pieces, *map(keep, weights), *accs, *factors]
    return pl.pallas_call(
        functools.partial(mid_kernel, block),
        out_shape=[
            shape(ROWS, 2 * HID, BF16),
            shape(ROWS + RANKS, 2 * HID, BF16),
            shape(RANKS, ROWS, F32),
            shape(RANKS, HID, F32),
        ],
        in_specs=[SM] + [VM] * (len(args) - 1),
        out_specs=[VM] * 4,
        scratch_shapes=[
            pltpu.VMEM((ROWS, HID), F32),
            pltpu.VMEM((ROWS, HID), F32),
            pltpu.VMEM((ROWS, HID), F32),
            pltpu.VMEM((RANKS, ROWS), F32),
            pltpu.VMEM((ROWS, HID), BF16),
            pltpu.VMEM((PIECE, FEATS), BF16),
        ],
        compiler_params=params(),
        cost_estimate=COST,
    )(*args)


def out_kernel(blocks, own, other, added, idx, *refs):
    refs = list(refs)
    wides = [refs.pop(0) for _ in range(own + other)]
    mine, theirs = refs[: 2 * own], refs[2 * own : 2 * own + other]
    refs = refs[2 * own + other :]
    before, outs = refs[: len(blocks)], refs[-len(blocks) :]
    for s, b in enumerate(blocks):
        terms = []
        if own:
            at = pl.ds(feature_at(idx, b), FEATS)
            terms += [(wides[0], w[at, :]) for w in mine]
        if other:
            at = 2 * BLOCKS.index(b) * FEATS
            terms += [(wides[-1], theirs[0][at + i * FEATS : at + (i + 1) * FEATS, :]) for i in range(2)]
        total = before[s][...] if added else None
        for i, (wide, w) in enumerate(terms):
            i = i % 2
            term = dot_nt(wide[0:ROWS, i * HID : (i + 1) * HID], w)
            total = term if total is None else total + term
        outs[s][...] = total.astype(outs[s].dtype)


def run_out(blocks, idx, wide, their, own_weights, their_weights, before, dtype):
    own, other, added = wide is not None, their is not None, before is not None
    args = [idx] + [wide] * own + [their] * other
    args += [keep(w) for w in (own_weights or ()) + ((their_weights,) if other else ())] + list(before or ())
    return pl.pallas_call(
        functools.partial(out_kernel, blocks, int(own), int(other), added),
        out_shape=[shape(ROWS, FEATS, dtype)] * len(blocks),
        in_specs=[SM] + [VM] * (len(args) - 1),
        out_specs=[VM] * len(blocks),
        compiler_params=params(),
        cost_estimate=COST,
    )(*args)


def rank_kernel(idx, ranks_out, their, out):
    at = pl.ds(pl.multiple_of(idx[2] * HALF, HALF), HALF)
    out[...] = ranks_out[:, at] + their[ROWS : ROWS + RANKS, at].astype(F32)


def chip_ranks(idx, ranks_out, their):
    return pl.pallas_call(
        rank_kernel,
        out_shape=shape(RANKS, HALF, F32),
        in_specs=[SM, VM, VM],
        out_specs=VM,
        compiler_params=params(),
        cost_estimate=COST,
    )(idx, ranks_out, their)


def finish_kernel(idx, mine, core, y, cross, x, dy, gif, uif, grads, adapter, ranks):
    halves = ((mine[...] + y[...].astype(F32)).astype(BF16), (core[...].astype(F32) + cross[...].astype(F32)).astype(BF16))
    for c in range(2):

        @pl.when(idx[2] == c)
        def _():
            ranks[:, c * HALF : (c + 1) * HALF] = halves[0]
            ranks[:, (1 - c) * HALF : (2 - c) * HALF] = halves[1]

    grads[0 : 2 * RANK, :] = SCALE * dot_nn(ranks[0 : 2 * RANK, :], x[...])
    grads[2 * RANK : RANKS, :] = SCALE * dot_nn(ranks[2 * RANK : RANKS, :], dy[...])
    adapter[...] = SCALE * (dot_tn(ranks[0:RANK, :], gif[...]) + dot_tn(ranks[RANK : 2 * RANK, :], uif[...]))


def finish(*args):
    return pl.pallas_call(
        finish_kernel,
        out_shape=[shape(RANKS, LANES, F32), shape(ROWS, LANES, F32)],
        in_specs=[SM] + [VM] * 8,
        out_specs=[VM] * 2,
        scratch_shapes=[pltpu.VMEM((RANKS, ROWS), BF16)],
        compiler_params=params(),
        cost_estimate=COST,
    )(*args)


def join(moving, here):
    return (moving.astype(F32) + here).astype(BF16)


def flip(v, axis, n, bits):
    return lax.ppermute(v, axis, [(i, i ^ bits) for i in range(n)])


def swap(v):
    return flip(v, "core", 2, 1)


def along(v):
    return lax.ppermute(v, ("z", "core"), [(2 * z + c, 2 * ((z + 1 - 2 * c) % ZN) + c) for z in range(ZN) for c in (0, 1)])


def after(v, done):
    return lax.optimization_barrier((v, done))[0]


def body(x, dy, wg, wu, wd, gif, gof, uif, uof, dif, dof):
    yhi, z, core = lax.axis_index("yhi"), lax.axis_index("z"), lax.axis_index("core")
    idx = jnp.stack([yhi, z, core]).astype(jnp.int32)
    first = core == 0

    own = pack(x, dy, gif, uif, dof)
    a0 = ordered(idx, own, swap(own))
    with jax.named_scope("y"):
        other = flip(after(own, a0), "yhi", 2, 1)
    with jax.named_scope("a1"):
        a1 = along(a0)
    with jax.named_scope("weights"):
        chosen = choose(idx, after(wg, a0), after(wu, a0))
        their_w = swap(chosen)
        weights = load(*(after(w, a0) for w in (wg, wu, wd)))
    other = after(other, (a1, chosen, weights))
    with jax.named_scope("swap_b0"):
        b0 = ordered(idx, other, swap(other))
    with jax.named_scope("b1"):
        b1 = along(b0)

    def acc(k, r, piece, accs):
        with jax.named_scope(f"swap_{'ab'[r]}{k}"):
            theirs = swap(piece)
        with jax.named_scope(f"acc_{'ab'[r]}{k}"):
            return run_acc(((-k, r), (k, r)), idx, (piece, theirs), weights, accs)

    with jax.named_scope("acc_0"):
        accs = run_acc(((0, 0), (0, 1)), idx, (a0, b0), weights, None)
    with jax.named_scope("a2"):
        a2 = along(a1)
    with jax.named_scope("b2"):
        b2 = along(after(b1, accs[3]))
    accs = acc(1, 0, a1, accs)
    with jax.named_scope("a3"):
        a3 = along(after(a2, accs[3]))
    accs = acc(1, 1, b1, accs)
    with jax.named_scope("b3"):
        b3 = along(after(b2, accs[3]))
    accs = acc(2, 0, a2, accs)
    accs = acc(2, 1, b2, accs)
    with jax.named_scope("a4"):
        a4 = along(half_of(idx, a3))
    with jax.named_scope("b4"):
        b4 = along(half_of(idx, b3))
    b3 = after(b3, accs[3])
    accs = acc(3, 0, a3, accs)
    accs = acc(3, 1, b3, accs)
    with jax.named_scope("swap_a4"):
        a4 = (a4, swap(after(a4, accs[3])))
    with jax.named_scope("acc_a4"):
        accs = run_part((4, 0), idx, a4, weights, accs)
    with jax.named_scope("swap_b4"):
        b4 = (b4, swap(b4))
    with jax.named_scope("mid"):
        wide, sent, ranks_out, grads = run_mid((4, 1), idx, b4, weights, accs, (gof, uof, dif))
    their = swap(sent)
    mine_w = tuple(weights[0:2])
    k1, k2, k3, k4 = (BLOCKS[i : i + 2] for i in range(0, 8, 2))
    with jax.named_scope("own_part"):
        part = run_out(k1 + k2, idx, wide, None, mine_w, None, None, F32)
    with jax.named_scope("out_1"):
        n4, f3 = run_out(k1, idx, None, their, None, their_w, part[0:2], BF16)
    with jax.named_scope("n1"):
        near = along(n4)
    with jax.named_scope("f1"):
        far = along(f3)
    with jax.named_scope("out_2"):
        n3, f2 = run_out(k2, idx, None, their, None, their_w, part[2:4], F32)
    with jax.named_scope("out_3"):
        n2, f1 = run_out(k3, idx, wide, their, mine_w, their_w, None, F32)
    with jax.named_scope("out_4"):
        n1, n0 = run_out(k4, idx, wide, their, mine_w, their_w, None, F32)

    def pair(name, v, axis, n, bits, done=None):
        sent = v.astype(BF16)
        with jax.named_scope(name):
            return v + flip(sent if done is None else after(sent, done), axis, n, bits).astype(F32)

    def total_rows(name, v, axis, n, bits, done=None):
        with jax.named_scope(name):
            return v + flip(v if done is None else after(v, done), axis, n, bits)

    def hop(name, v):
        with jax.named_scope(name):
            return along(v)

    with jax.named_scope("ranks"):
        ranks = chip_ranks(idx, after(ranks_out, n4), their)
    ranks = pair("ranks_1", ranks, "z", ZN, 1)
    near_2, far_2 = join(near, after(n3, f1)), join(far, f2)
    near, far = hop("n2", near_2), hop("f2", far_2)
    grads = total_rows("out_x1", grads, "x", 4, 1, n4)
    ranks = pair("ranks_2", ranks, "z", ZN, 2, near_2)
    near_3, far_3 = join(near, after(n2, n0)), join(far, f1)
    near, far = hop("n3", near_3), hop("f3", far_3)
    grads = total_rows("out_x2", grads, "x", 4, 2)
    ranks = pair("ranks_4", ranks, "z", ZN, 4, (near_3, grads))
    near = hop("n4", join(near, n1))
    grads = total_rows("out_y", grads, "ylo", 2, 1)
    with jax.named_scope("far_core"):
        far = swap(after(far, near))
    sent = after(ranks.astype(BF16), grads)
    with jax.named_scope("ranks_core"):
        by_core = swap(sent)
    with jax.named_scope("ranks_y"):
        by_y = flip(sent, "yhi", 2, 1)
    with jax.named_scope("ranks_cross"):
        by_cross = flip(sent, ("yhi", "core"), 4, 3)
    with jax.named_scope("in_grads"):
        in_grads, adapter = finish(idx, ranks, by_core, by_y, by_cross, x, dy, gif, uif)
    in_grads = total_rows("in_x1", in_grads, "x", 4, 1, far)
    in_grads = total_rows("in_x2", in_grads, "x", 4, 2)
    in_grads = total_rows("in_y", in_grads, "ylo", 2, 1)

    total = n0 + near.astype(F32) + far.astype(F32)
    low, high = total[:, 0:LANES], total[:, LANES:FEATS]
    cross = [(0, 1), (1, 2), (2, 3), (3, 0)]
    got = lax.ppermute(jnp.where(first, high, low).astype(BF16), ("yhi", "core"), cross)
    more = lax.ppermute(high.astype(BF16), ("yhi", "core"), [(1, 3), (3, 1), (0, 0), (2, 2)])
    rows_grad = got.astype(F32) + jnp.where(first, low, more.astype(F32)) + adapter
    g = [in_grads[i * RANK : (i + 1) * RANK] for i in range(3)]
    o = [grads[i * RANK : (i + 1) * RANK] for i in range(3)]
    return rows_grad.astype(BF16), g[0], o[0], g[1], o[1], o[2], g[2]


def solution(mesh):
    split = Mesh(mesh.devices.reshape(2, 4, 2, 8, 2), ("ylo", "x", "yhi", "z", "core"))
    dp, tensor = ("ylo", "x"), ("yhi", "z", "core")
    cols = P(None, tensor)
    return jax.shard_map(
        body,
        mesh=split,
        in_specs=(P(dp, tensor), P(dp, tensor), cols, cols, P(tensor, None), cols, cols, cols, cols, cols, cols),
        out_specs=(P(dp, tensor), cols, cols, cols, cols, cols, cols),
        check_vma=False,
    )
```

```python
import functools

import jax
import jax.numpy as jnp
from jax import lax
from jax.experimental import pallas as pl
from jax.experimental.pallas import tpu as pltpu
from jax.sharding import Mesh, PartitionSpec as P

SCALE = 0.5
ROWS = 512
HALF = ROWS // 2
LANES = 128
FEATS = 2 * LANES
HID = 512
RANK = 32
RANKS = 3 * RANK
PIECE = 2 * ROWS + RANKS
PART = PIECE // 2
RIDERS = 2 * RANKS
ZN = 8
VMEM_LIMIT = 8 * 1024 * 1024
F32 = jnp.float32
BF16 = jnp.bfloat16

VM = pl.BlockSpec(memory_space=pltpu.VMEM)
SM = pl.BlockSpec(memory_space=pltpu.SMEM)
COST = pl.CostEstimate(flops=1, bytes_accessed=1, transcendentals=0)
ACC_COST = COST
PART_COST = pl.CostEstimate(flops=8 * 10**9, bytes_accessed=1, transcendentals=0)


def dot_nn(a, b):
    return lax.dot_general(a, b, (((1,), (0,)), ((), ())), preferred_element_type=F32)


def dot_nt(a, b):
    return lax.dot_general(a, b, (((1,), (1,)), ((), ())), preferred_element_type=F32)


def dot_tn(a, b):
    return lax.dot_general(a, b, (((0,), (0,)), ((), ())), preferred_element_type=F32)


def feature_at(idx, block):
    k, r = block
    core = idx[2]
    r = {"near": core, "far": 1 - core}.get(r, r)
    yhi = lax.rem(idx[0] + r, 2)
    z = lax.rem(idx[1] + k * (1 - 2 * core) + ZN, ZN)
    return pl.multiple_of((yhi * ZN + z) * FEATS, FEATS)


def params():
    return pltpu.CompilerParams(vmem_limit_bytes=VMEM_LIMIT)


def keep(v):
    return pltpu.with_memory_space_constraint(v, pltpu.VMEM)


def stay(v):
    return pltpu.with_memory_space_constraint(v, pltpu.HBM)


def shape(rows, cols, dtype):
    return jax.ShapeDtypeStruct((rows, cols), dtype)


def pack_kernel(x, dy, gif, uif, dof, out, sem):
    at, copies = 0, []
    for i, ref in enumerate((x, dy, gif, uif, dof)):
        rows = ref.shape[0]
        copies.append(pltpu.make_async_copy(ref, out.at[at : at + rows, :], sem.at[i]))
        at += rows
    for c in copies:
        c.start()
    for c in copies:
        c.wait()


def pack(*arrays):
    return pl.pallas_call(
        pack_kernel,
        out_shape=shape(PIECE, LANES, BF16),
        in_specs=[pl.BlockSpec(memory_space=pl.ANY)] * 5,
        out_specs=VM,
        scratch_shapes=[pltpu.SemaphoreType.DMA((5,))],
        compiler_params=params(),
        cost_estimate=COST,
    )(*map(stay, arrays))


def load_kernel(*refs):
    n = len(refs) // 2
    ins, outs, sem = refs[:n], refs[n : 2 * n], refs[2 * n]
    copies = [pltpu.make_async_copy(a, b, sem.at[i]) for i, (a, b) in enumerate(zip(ins, outs))]
    for c in copies:
        c.start()
    for c in copies:
        c.wait()


def load(*arrays):
    return pl.pallas_call(
        load_kernel,
        out_shape=[jax.ShapeDtypeStruct(a.shape, a.dtype) for a in arrays],
        in_specs=[pl.BlockSpec(memory_space=pl.ANY)] * len(arrays),
        out_specs=[VM] * len(arrays),
        scratch_shapes=[pltpu.SemaphoreType.DMA((len(arrays),))],
        compiler_params=params(),
        cost_estimate=COST,
    )(*map(stay, arrays))


BLOCKS = ((4, "near"), (3, "far"), (3, "near"), (2, "far"), (2, "near"), (1, "far"), (1, "near"), (0, "near"))


def choose_kernel(idx, wg, wu, out, sem):
    other = (idx[0], idx[1], 1 - idx[2])
    copies = []
    for s, b in enumerate(BLOCKS):
        at = pl.ds(feature_at(other, b), FEATS)
        for i, w in enumerate((wg, wu)):
            to = out.at[pl.ds((2 * s + i) * FEATS, FEATS), :]
            copies.append(pltpu.make_async_copy(w.at[at, :], to, sem.at[s, i]))
    for c in copies:
        c.start()
    for c in copies:
        c.wait()


def choose(idx, wg, wu):
    return pl.pallas_call(
        choose_kernel,
        out_shape=shape(2 * len(BLOCKS) * FEATS, HID, BF16),
        in_specs=[SM] + [pl.BlockSpec(memory_space=pl.ANY)] * 2,
        out_specs=VM,
        scratch_shapes=[pltpu.SemaphoreType.DMA((len(BLOCKS), 2))],
        compiler_params=params(),
        cost_estimate=COST,
    )(idx, stay(wg), stay(wu))


def ordered_kernel(idx, mine, theirs, out):
    @pl.when(idx[2] == 0)
    def _():
        out[:, 0:LANES] = mine[...]
        out[:, LANES:FEATS] = theirs[...]

    @pl.when(idx[2] != 0)
    def _():
        out[:, 0:LANES] = theirs[...]
        out[:, LANES:FEATS] = mine[...]


def ordered(idx, mine, theirs):
    return pl.pallas_call(
        ordered_kernel,
        out_shape=shape(PIECE, FEATS, BF16),
        in_specs=[SM, VM, VM],
        out_specs=VM,
        compiler_params=params(),
        cost_estimate=COST,
    )(idx, mine, theirs)


def accumulate(blocks, first, idx, pieces, weights, accs, outs):
    wg, wu, wd = weights
    at = [feature_at(idx, b) for b in blocks]
    x, c, f = (
        jnp.concatenate([p[lo:hi, :] for p in pieces], axis=1)
        for lo, hi in ((0, ROWS), (ROWS, 2 * ROWS), (2 * ROWS, PIECE))
    )

    def put(i, sl, val):
        outs[i][sl] = val if first else accs[i][sl] + val

    put(0, Ellipsis, dot_nn(x, jnp.concatenate([wg[pl.ds(a, FEATS), :] for a in at], axis=0)))
    put(1, Ellipsis, dot_nn(x, jnp.concatenate([wu[pl.ds(a, FEATS), :] for a in at], axis=0)))
    put(2, Ellipsis, dot_nt(c, jnp.concatenate([wd[:, pl.ds(a, FEATS)] for a in at], axis=1)))
    put(3, (slice(0, 2 * RANK), slice(None)), dot_nt(f[0 : 2 * RANK], x))
    put(3, (slice(2 * RANK, RANKS), slice(None)), dot_nt(f[2 * RANK : RANKS], c))


def acc_kernel(blocks, first, idx, p0, p1, wg, wu, wd, *refs):
    accs, outs = (None, refs) if first else (refs[:4], refs[4:])
    accumulate(blocks, first, idx, (p0, p1), (wg, wu, wd), accs, outs)


ACC_SHAPES = [shape(ROWS, HID, F32)] * 3 + [shape(RANKS, ROWS, F32)]


def run_acc(blocks, idx, pieces, weights, accs):
    first = accs is None
    args = [idx, *pieces, *map(keep, weights)] + ([] if first else list(accs))
    aliases = {} if first else {len(args) - 4 + i: i for i in range(4)}
    return pl.pallas_call(
        functools.partial(acc_kernel, blocks, first),
        out_shape=ACC_SHAPES,
        in_specs=[SM] + [VM] * (len(args) - 1),
        out_specs=[VM] * 4,
        input_output_aliases=aliases,
        compiler_params=params(),
        cost_estimate=ACC_COST,
    )(*args)


def joined(idx, mine, theirs, whole):
    at = pl.multiple_of(idx[2] * PART, PART)
    whole[pl.ds(at, PART), :] = mine[...]
    whole[pl.ds(PART - at, PART), :] = theirs[...]
    return whole


def part_kernel(block, idx, mine, theirs, wg, wu, wd, *refs):
    accs, outs, whole = refs[:4], refs[4:8], refs[8]
    accumulate((block,), False, idx, (joined(idx, mine, theirs, whole),), (wg, wu, wd), accs, outs)


def run_part(block, idx, pieces, weights, accs):
    args = [idx, *pieces, *map(keep, weights), *accs]
    return pl.pallas_call(
        functools.partial(part_kernel, block),
        out_shape=ACC_SHAPES,
        in_specs=[SM] + [VM] * (len(args) - 1),
        out_specs=[VM] * 4,
        scratch_shapes=[pltpu.VMEM((PIECE, FEATS), BF16)],
        input_output_aliases={len(args) - 4 + i: i for i in range(4)},
        compiler_params=params(),
        cost_estimate=PART_COST,
    )(*args)


def half_kernel(idx, piece, out):
    out[...] = piece[pl.ds(pl.multiple_of(idx[2] * PART, PART), PART), :]


def half_of(idx, piece):
    return pl.pallas_call(
        half_kernel,
        out_shape=shape(PART, FEATS, BF16),
        in_specs=[SM, VM],
        out_specs=VM,
        compiler_params=params(),
        cost_estimate=COST,
    )(idx, piece)


def mid_kernel(block, idx, mine, theirs, wg, wu, wd, *refs):
    accs, (gof, uof, dif), (out, sent, ranks_out, grads), (g, u, h, rt, hid, whole) = (
        refs[:4],
        refs[4:7],
        refs[7:11],
        refs[11:17],
    )
    accumulate((block,), False, idx, (joined(idx, mine, theirs, whole),), (wg, wu, wd), accs, (g, u, h, rt))
    ranks = rt[...].astype(BF16)
    for i, (ref, fac) in enumerate(((g, gof), (u, uof), (h, dif))):
        ref[...] += SCALE * dot_tn(ranks[i * RANK : (i + 1) * RANK], fac[...])
    step = 64

    @pl.loop(0, ROWS // step)
    def _(i):
        at = pl.ds(pl.multiple_of(i * step, step), step)
        gate, up, grad = g[at, :], u[at, :], h[at, :]
        sig = jax.nn.sigmoid(gate)
        act = gate * sig
        hid[at, :] = (act * up).astype(BF16)
        gate_grad = (grad * up * sig * (1.0 + gate * (1.0 - sig))).astype(BF16)
        up_grad = (grad * act).astype(BF16)
        for ref in (out, sent):
            ref[at, 0:HID] = gate_grad
            ref[at, HID : 2 * HID] = up_grad

    three = (out[0:ROWS, 0:HID], out[0:ROWS, HID : 2 * HID], hid[...])
    for i, (val, fac) in enumerate(zip(three, (gof, uof, dif))):
        at = slice(i * RANK, (i + 1) * RANK)
        ranks_out[at, :] = dot_nt(fac[...], val)
        grads[at, :] = SCALE * dot_nn(ranks[at], val)
    sent[ROWS : ROWS + RANKS, 0:HID] = ranks_out[...].astype(BF16)
    sent[ROWS : ROWS + RANKS, HID : 2 * HID] = jnp.zeros((RANKS, HID), BF16)


def run_mid(block, idx, pieces, weights, accs, factors):
    args = [idx, *pieces, *map(keep, weights), *accs, *factors]
    return pl.pallas_call(
        functools.partial(mid_kernel, block),
        out_shape=[
            shape(ROWS, 2 * HID, BF16),
            shape(ROWS + RANKS, 2 * HID, BF16),
            shape(RANKS, ROWS, F32),
            shape(RANKS, HID, F32),
        ],
        in_specs=[SM] + [VM] * (len(args) - 1),
        out_specs=[VM] * 4,
        scratch_shapes=[
            pltpu.VMEM((ROWS, HID), F32),
            pltpu.VMEM((ROWS, HID), F32),
            pltpu.VMEM((ROWS, HID), F32),
            pltpu.VMEM((RANKS, ROWS), F32),
            pltpu.VMEM((ROWS, HID), BF16),
            pltpu.VMEM((PIECE, FEATS), BF16),
        ],
        compiler_params=params(),
        cost_estimate=COST,
    )(*args)


def out_kernel(blocks, own, other, added, idx, *refs):
    refs = list(refs)
    wides = [refs.pop(0) for _ in range(own + other)]
    mine, theirs = refs[: 2 * own], refs[2 * own : 2 * own + other]
    refs = refs[2 * own + other :]
    before, outs = refs[: len(blocks)], refs[-len(blocks) :]
    for s, b in enumerate(blocks):
        terms = []
        if own:
            at = pl.ds(feature_at(idx, b), FEATS)
            terms += [(wides[0], w[at, :]) for w in mine]
        if other:
            at = 2 * BLOCKS.index(b) * FEATS
            terms += [(wides[-1], theirs[0][at + i * FEATS : at + (i + 1) * FEATS, :]) for i in range(2)]
        total = before[s][...] if added else None
        for i, (wide, w) in enumerate(terms):
            i = i % 2
            term = dot_nt(wide[0:ROWS, i * HID : (i + 1) * HID], w)
            total = term if total is None else total + term
        outs[s][...] = total.astype(outs[s].dtype)


def run_out(blocks, idx, wide, their, own_weights, their_weights, before, dtype):
    own, other, added = wide is not None, their is not None, before is not None
    args = [idx] + [wide] * own + [their] * other
    args += [keep(w) for w in (own_weights or ()) + ((their_weights,) if other else ())] + list(before or ())
    return pl.pallas_call(
        functools.partial(out_kernel, blocks, int(own), int(other), added),
        out_shape=[shape(ROWS, FEATS, dtype)] * len(blocks),
        in_specs=[SM] + [VM] * (len(args) - 1),
        out_specs=[VM] * len(blocks),
        compiler_params=params(),
        cost_estimate=COST,
    )(*args)


def first_kernel(idx, their, weights, ranks_out, p0, p1, near, far, ranks):
    for s, (p, out) in enumerate(((p0, near), (p1, far))):
        total = p[...]
        for i in range(2):
            at = (2 * s + i) * FEATS
            total = total + dot_nt(their[0:ROWS, i * HID : (i + 1) * HID], weights[at : at + FEATS, :])
        out[0:ROWS, :] = total.astype(BF16)
    for i in range(2):
        lanes, rows = slice(i * HALF, (i + 1) * HALF), slice(i * RANKS, (i + 1) * RANKS)
        chip = ranks_out[:, lanes] + their[ROWS : ROWS + RANKS, lanes].astype(F32)
        ranks[rows, :] = jnp.where(idx[2] == 0, chip, 0.0)
        near[ROWS + i * RANKS : ROWS + (i + 1) * RANKS, :] = chip.astype(BF16)


def first_out(idx, their, weights, ranks_out, parts):
    return pl.pallas_call(
        first_kernel,
        out_shape=[shape(ROWS + RIDERS, FEATS, BF16), shape(ROWS, FEATS, BF16), shape(RIDERS, FEATS, F32)],
        in_specs=[SM] + [VM] * 5,
        out_specs=[VM] * 3,
        compiler_params=params(),
        cost_estimate=COST,
    )(idx, their, keep(weights), ranks_out, *parts)


def ride_kernel(moving, here, ranks, out, ranks_now):
    out[0:ROWS, :] = (moving[0:ROWS, :].astype(F32) + here[...]).astype(BF16)
    riders = moving[ROWS : ROWS + RIDERS, :]
    out[ROWS : ROWS + RIDERS, :] = riders
    ranks_now[...] = ranks[...] + riders.astype(F32)


def ride(moving, here, ranks):
    return pl.pallas_call(
        ride_kernel,
        out_shape=[shape(ROWS + RIDERS, FEATS, BF16), shape(RIDERS, FEATS, F32)],
        in_specs=[VM] * 3,
        out_specs=[VM] * 2,
        compiler_params=params(),
        cost_estimate=COST,
    )(moving, here, ranks)


def finish_kernel(idx, mine, theirs, a0, b0, grads, adapter, ranks):
    for i in range(2):
        rows = slice(i * RANKS, (i + 1) * RANKS)
        ranks[:, i * HALF : (i + 1) * HALF] = (mine[rows, :] + theirs[rows, :].astype(F32)).astype(BF16)
    lanes = pl.ds(pl.multiple_of(idx[2] * LANES, LANES), LANES)
    for i, piece in enumerate((a0, b0)):
        at = i * RANKS
        grads[at : at + 2 * RANK, :] = SCALE * dot_nn(ranks[0 : 2 * RANK, :], piece[0:ROWS, lanes])
        grads[at + 2 * RANK : at + RANKS, :] = SCALE * dot_nn(ranks[2 * RANK : RANKS, :], piece[ROWS : 2 * ROWS, lanes])

        @pl.when(idx[2] == i)
        def _():
            adapter[...] = SCALE * dot_tn(ranks[0 : 2 * RANK, :], piece[2 * ROWS : 2 * ROWS + 2 * RANK, :])


def finish(*args):
    return pl.pallas_call(
        finish_kernel,
        out_shape=[shape(2 * RANKS, LANES, F32), shape(ROWS, FEATS, F32)],
        in_specs=[SM] + [VM] * 4,
        out_specs=[VM] * 2,
        scratch_shapes=[pltpu.VMEM((RANKS, ROWS), BF16)],
        compiler_params=params(),
        cost_estimate=COST,
    )(*args)


def join(moving, here):
    return (moving.astype(F32) + here).astype(BF16)


def flip(v, axis, n, bits):
    return lax.ppermute(v, axis, [(i, i ^ bits) for i in range(n)])


def swap(v):
    return flip(v, "core", 2, 1)


def along(v):
    return lax.ppermute(v, ("z", "core"), [(2 * z + c, 2 * ((z + 1 - 2 * c) % ZN) + c) for z in range(ZN) for c in (0, 1)])


def after(v, done):
    return lax.optimization_barrier((v, done))[0]


def body(x, dy, wg, wu, wd, gif, gof, uif, uof, dif, dof):
    yhi, z, core = lax.axis_index("yhi"), lax.axis_index("z"), lax.axis_index("core")
    idx = jnp.stack([yhi, z, core]).astype(jnp.int32)
    first = core == 0

    own = pack(x, dy, gif, uif, dof)
    a0 = ordered(idx, own, swap(own))
    with jax.named_scope("y"):
        other = flip(after(own, a0), "yhi", 2, 1)
    with jax.named_scope("a1"):
        a1 = along(a0)
    with jax.named_scope("weights"):
        chosen = choose(idx, after(wg, a0), after(wu, a0))
        their_w = swap(chosen)
        weights = load(*(after(w, a0) for w in (wg, wu, wd)))
    other = after(other, (a1, chosen, weights))
    with jax.named_scope("swap_b0"):
        b0 = ordered(idx, other, swap(other))
    with jax.named_scope("b1"):
        b1 = along(b0)

    def acc(k, r, piece, accs):
        with jax.named_scope(f"swap_{'ab'[r]}{k}"):
            theirs = swap(piece)
        with jax.named_scope(f"acc_{'ab'[r]}{k}"):
            return run_acc(((-k, r), (k, r)), idx, (piece, theirs), weights, accs)

    with jax.named_scope("acc_0"):
        accs = run_acc(((0, 0), (0, 1)), idx, (a0, b0), weights, None)
    with jax.named_scope("a2"):
        a2 = along(a1)
    with jax.named_scope("b2"):
        b2 = along(after(b1, accs[3]))
    accs = acc(1, 0, a1, accs)
    with jax.named_scope("a3"):
        a3 = along(after(a2, accs[3]))
    accs = acc(1, 1, b1, accs)
    with jax.named_scope("b3"):
        b3 = along(b2)
    accs = acc(2, 0, a2, accs)
    accs = acc(2, 1, b2, accs)
    with jax.named_scope("a4"):
        a4 = along(half_of(idx, a3))
    with jax.named_scope("b4"):
        b4 = along(half_of(idx, b3))
    b3 = after(b3, accs[3])
    accs = acc(3, 0, a3, accs)
    accs = acc(3, 1, b3, accs)
    with jax.named_scope("swap_a4"):
        a4 = (a4, swap(after(a4, accs[3])))
    with jax.named_scope("acc_a4"):
        accs = run_part((4, 0), idx, a4, weights, accs)
    with jax.named_scope("swap_b4"):
        b4 = (b4, swap(b4))
    with jax.named_scope("mid"):
        wide, sent, ranks_out, grads = run_mid((4, 1), idx, b4, weights, accs, (gof, uof, dif))
    their = swap(sent)
    mine_w = tuple(weights[0:2])
    k1, k2, k3, k4 = (BLOCKS[i : i + 2] for i in range(0, 8, 2))
    with jax.named_scope("own_part"):
        part = run_out(k1 + k2, idx, wide, None, mine_w, None, None, F32)
    with jax.named_scope("out_1"):
        n4, f3, ranks = first_out(idx, their, their_w, ranks_out, part[0:2])
    with jax.named_scope("n1"):
        near = along(n4)
    with jax.named_scope("f1"):
        far = along(f3)
    with jax.named_scope("out_2"):
        n3, f2 = run_out(k2, idx, None, their, None, their_w, part[2:4], F32)
    with jax.named_scope("out_3"):
        n2, f1 = run_out(k3, idx, wide, their, mine_w, their_w, None, F32)
    with jax.named_scope("out_4"):
        n1, n0 = run_out(k4, idx, wide, their, mine_w, their_w, None, F32)

    def hop(name, v):
        with jax.named_scope(name):
            return along(v)

    def total_rows(name, v, axis, n, bits):
        with jax.named_scope(name):
            return v + flip(v, axis, n, bits)

    def sum_x(name, v, sent):
        with jax.named_scope(name):
            other = [flip(sent, "x", 4, bits) for bits in (1, 2, 3)]
            return (v + other[0]) + (other[1] + other[2])

    near, ranks = ride(near, after(n3, f1), ranks)
    far = join(far, f2)
    near, far = hop("n2", near), hop("f2", far)
    near, ranks = ride(near, after(n2, n0), ranks)
    far = join(far, f1)
    near, far = hop("n3", near), hop("f3", far)
    near, ranks = ride(near, n1, ranks)
    near = hop("n4", near)
    grads = sum_x("out_x", grads, grads)
    ranks = ranks + jnp.where(first, near[ROWS:].astype(F32), 0.0)
    with jax.named_scope("far_core"):
        far = swap(far)
    with jax.named_scope("ranks_core"):
        by_core = swap(after(ranks.astype(BF16), (far, grads)))
    grads = total_rows("out_y", grads, "ylo", 2, 1)
    with jax.named_scope("in_grads"):
        in_grads, adapter = finish(idx, ranks, by_core, a0, b0)
    in_grads = sum_x("in_x", in_grads, in_grads)

    total = n0 + near[0:ROWS].astype(F32) + far.astype(F32) + adapter
    low, high = total[:, 0:LANES], total[:, LANES:FEATS]
    cross = [(0, 1), (1, 2), (2, 3), (3, 0)]
    with jax.named_scope("got"):
        got = lax.ppermute(jnp.where(first, high, low).astype(BF16), ("yhi", "core"), cross)
        more = lax.ppermute(high.astype(BF16), ("yhi", "core"), [(1, 3), (3, 1), (0, 0), (2, 2)])
    rows_grad = got.astype(F32) + jnp.where(first, low, more.astype(F32))
    with jax.named_scope("in_y"):
        here, there = after(in_grads[0:RANKS], (grads, got, more)), in_grads[RANKS:]
        in_grads = (here + flip(here, "ylo", 2, 1)) + (
            flip(there, "yhi", 2, 1) + flip(there, ("ylo", "yhi"), 4, 3)
        )
    g = [in_grads[i * RANK : (i + 1) * RANK] for i in range(3)]
    o = [grads[i * RANK : (i + 1) * RANK] for i in range(3)]
    return rows_grad.astype(BF16), g[0], o[0], g[1], o[1], o[2], g[2]


def solution(mesh):
    split = Mesh(mesh.devices.reshape(2, 4, 2, 8, 2), ("ylo", "x", "yhi", "z", "core"))
    dp, tensor = ("ylo", "x"), ("yhi", "z", "core")
    cols = P(None, tensor)
    return jax.shard_map(
        body,
        mesh=split,
        in_specs=(P(dp, tensor), P(dp, tensor), cols, cols, P(tensor, None), cols, cols, cols, cols, cols, cols),
        out_specs=(P(dp, tensor), cols, cols, cols, cols, cols, cols),
        check_vma=False,
    )
```

```python
import functools

import jax
import jax.numpy as jnp
from jax import lax
from jax.experimental import pallas as pl
from jax.experimental.pallas import tpu as pltpu
from jax.sharding import Mesh, PartitionSpec as P

SCALE = 0.5
ROWS = 512
HALF = ROWS // 2
LANES = 128
FEATS = 2 * LANES
HID = 512
RANK = 32
RANKS = 3 * RANK
PIECE = 2 * ROWS + RANKS
PART = PIECE // 2
RIDERS = 2 * RANKS
ZN = 8
VMEM_LIMIT = 8 * 1024 * 1024
F32 = jnp.float32
BF16 = jnp.bfloat16

VM = pl.BlockSpec(memory_space=pltpu.VMEM)
SM = pl.BlockSpec(memory_space=pltpu.SMEM)
COST = pl.CostEstimate(flops=1, bytes_accessed=1, transcendentals=0)
ACC_COST = COST
PART_COST = pl.CostEstimate(flops=8 * 10**9, bytes_accessed=1, transcendentals=0)


def dot_nn(a, b):
    return lax.dot_general(a, b, (((1,), (0,)), ((), ())), preferred_element_type=F32)


def dot_nt(a, b):
    return lax.dot_general(a, b, (((1,), (1,)), ((), ())), preferred_element_type=F32)


def dot_tn(a, b):
    return lax.dot_general(a, b, (((0,), (0,)), ((), ())), preferred_element_type=F32)


def feature_at(idx, block):
    k, r = block
    core = idx[2]
    r = {"near": core, "far": 1 - core}.get(r, r)
    yhi = lax.rem(idx[0] + r, 2)
    z = lax.rem(idx[1] + k * (1 - 2 * core) + ZN, ZN)
    return pl.multiple_of((yhi * ZN + z) * FEATS, FEATS)


def params():
    return pltpu.CompilerParams(vmem_limit_bytes=VMEM_LIMIT)


def keep(v):
    return pltpu.with_memory_space_constraint(v, pltpu.VMEM)


def stay(v):
    return pltpu.with_memory_space_constraint(v, pltpu.HBM)


def shape(rows, cols, dtype):
    return jax.ShapeDtypeStruct((rows, cols), dtype)


def pack_kernel(x, dy, gif, uif, dof, out, sem):
    at, copies = 0, []
    for i, ref in enumerate((x, dy, gif, uif, dof)):
        rows = ref.shape[0]
        copies.append(pltpu.make_async_copy(ref, out.at[at : at + rows, :], sem.at[i]))
        at += rows
    for c in copies:
        c.start()
    for c in copies:
        c.wait()


def pack(*arrays):
    return pl.pallas_call(
        pack_kernel,
        out_shape=shape(PIECE, LANES, BF16),
        in_specs=[pl.BlockSpec(memory_space=pl.ANY)] * 5,
        out_specs=VM,
        scratch_shapes=[pltpu.SemaphoreType.DMA((5,))],
        compiler_params=params(),
        cost_estimate=COST,
    )(*map(stay, arrays))


def load_kernel(*refs):
    n = len(refs) // 2
    ins, outs, sem = refs[:n], refs[n : 2 * n], refs[2 * n]
    copies = [pltpu.make_async_copy(a, b, sem.at[i]) for i, (a, b) in enumerate(zip(ins, outs))]
    for c in copies:
        c.start()
    for c in copies:
        c.wait()


def load(*arrays):
    return pl.pallas_call(
        load_kernel,
        out_shape=[jax.ShapeDtypeStruct(a.shape, a.dtype) for a in arrays],
        in_specs=[pl.BlockSpec(memory_space=pl.ANY)] * len(arrays),
        out_specs=[VM] * len(arrays),
        scratch_shapes=[pltpu.SemaphoreType.DMA((len(arrays),))],
        compiler_params=params(),
        cost_estimate=COST,
    )(*map(stay, arrays))


BLOCKS = ((4, "near"), (3, "far"), (3, "near"), (2, "far"), (2, "near"), (1, "far"), (1, "near"), (0, "near"))


def choose_kernel(idx, wg, wu, out, sem):
    other = (idx[0], idx[1], 1 - idx[2])
    copies = []
    for s, b in enumerate(BLOCKS):
        at = pl.ds(feature_at(other, b), FEATS)
        for i, w in enumerate((wg, wu)):
            to = out.at[pl.ds((2 * s + i) * FEATS, FEATS), :]
            copies.append(pltpu.make_async_copy(w.at[at, :], to, sem.at[s, i]))
    for c in copies:
        c.start()
    for c in copies:
        c.wait()


def choose(idx, wg, wu):
    return pl.pallas_call(
        choose_kernel,
        out_shape=shape(2 * len(BLOCKS) * FEATS, HID, BF16),
        in_specs=[SM] + [pl.BlockSpec(memory_space=pl.ANY)] * 2,
        out_specs=VM,
        scratch_shapes=[pltpu.SemaphoreType.DMA((len(BLOCKS), 2))],
        compiler_params=params(),
        cost_estimate=COST,
    )(idx, stay(wg), stay(wu))


def ordered_kernel(idx, mine, theirs, out):
    @pl.when(idx[2] == 0)
    def _():
        out[:, 0:LANES] = mine[...]
        out[:, LANES:FEATS] = theirs[...]

    @pl.when(idx[2] != 0)
    def _():
        out[:, 0:LANES] = theirs[...]
        out[:, LANES:FEATS] = mine[...]


def ordered(idx, mine, theirs):
    return pl.pallas_call(
        ordered_kernel,
        out_shape=shape(PIECE, FEATS, BF16),
        in_specs=[SM, VM, VM],
        out_specs=VM,
        compiler_params=params(),
        cost_estimate=COST,
    )(idx, mine, theirs)


def accumulate(blocks, first, idx, pieces, weights, accs, outs):
    wg, wu, wd = weights
    at = [feature_at(idx, b) for b in blocks]
    x, c, f = (
        jnp.concatenate([p[lo:hi, :] for p in pieces], axis=1)
        for lo, hi in ((0, ROWS), (ROWS, 2 * ROWS), (2 * ROWS, PIECE))
    )

    def put(i, sl, val):
        outs[i][sl] = val if first else accs[i][sl] + val

    put(0, Ellipsis, dot_nn(x, jnp.concatenate([wg[pl.ds(a, FEATS), :] for a in at], axis=0)))
    put(1, Ellipsis, dot_nn(x, jnp.concatenate([wu[pl.ds(a, FEATS), :] for a in at], axis=0)))
    put(2, Ellipsis, dot_nt(c, jnp.concatenate([wd[:, pl.ds(a, FEATS)] for a in at], axis=1)))
    put(3, (slice(0, 2 * RANK), slice(None)), dot_nt(f[0 : 2 * RANK], x))
    put(3, (slice(2 * RANK, RANKS), slice(None)), dot_nt(f[2 * RANK : RANKS], c))


def acc_kernel(blocks, first, idx, p0, p1, wg, wu, wd, *refs):
    accs, outs = (None, refs) if first else (refs[:4], refs[4:])
    accumulate(blocks, first, idx, (p0, p1), (wg, wu, wd), accs, outs)


ACC_SHAPES = [shape(ROWS, HID, F32)] * 3 + [shape(RANKS, ROWS, F32)]


def run_acc(blocks, idx, pieces, weights, accs):
    first = accs is None
    args = [idx, *pieces, *map(keep, weights)] + ([] if first else list(accs))
    aliases = {} if first else {len(args) - 4 + i: i for i in range(4)}
    return pl.pallas_call(
        functools.partial(acc_kernel, blocks, first),
        out_shape=ACC_SHAPES,
        in_specs=[SM] + [VM] * (len(args) - 1),
        out_specs=[VM] * 4,
        input_output_aliases=aliases,
        compiler_params=params(),
        cost_estimate=ACC_COST,
    )(*args)


def joined(idx, mine, theirs, whole):
    at = pl.multiple_of(idx[2] * PART, PART)
    whole[pl.ds(at, PART), :] = mine[...]
    whole[pl.ds(PART - at, PART), :] = theirs[...]
    return whole


def part_kernel(block, idx, mine, theirs, wg, wu, wd, *refs):
    accs, outs, whole = refs[:4], refs[4:8], refs[8]
    accumulate((block,), False, idx, (joined(idx, mine, theirs, whole),), (wg, wu, wd), accs, outs)


def run_part(block, idx, pieces, weights, accs):
    args = [idx, *pieces, *map(keep, weights), *accs]
    return pl.pallas_call(
        functools.partial(part_kernel, block),
        out_shape=ACC_SHAPES,
        in_specs=[SM] + [VM] * (len(args) - 1),
        out_specs=[VM] * 4,
        scratch_shapes=[pltpu.VMEM((PIECE, FEATS), BF16)],
        input_output_aliases={len(args) - 4 + i: i for i in range(4)},
        compiler_params=params(),
        cost_estimate=PART_COST,
    )(*args)


def half_kernel(idx, piece, out):
    out[...] = piece[pl.ds(pl.multiple_of(idx[2] * PART, PART), PART), :]


def half_of(idx, piece):
    return pl.pallas_call(
        half_kernel,
        out_shape=shape(PART, FEATS, BF16),
        in_specs=[SM, VM],
        out_specs=VM,
        compiler_params=params(),
        cost_estimate=COST,
    )(idx, piece)


def mid_kernel(block, idx, mine, theirs, wg, wu, wd, *refs):
    accs, (gof, uof, dif), (out, sent, ranks_out, grads), (g, u, h, rt, hid, whole) = (
        refs[:4],
        refs[4:7],
        refs[7:11],
        refs[11:17],
    )
    accumulate((block,), False, idx, (joined(idx, mine, theirs, whole),), (wg, wu, wd), accs, (g, u, h, rt))
    ranks = rt[...].astype(BF16)
    for i, (ref, fac) in enumerate(((g, gof), (u, uof), (h, dif))):
        ref[...] += SCALE * dot_tn(ranks[i * RANK : (i + 1) * RANK], fac[...])
    step = 64

    @pl.loop(0, ROWS // step)
    def _(i):
        at = pl.ds(pl.multiple_of(i * step, step), step)
        gate, up, grad = g[at, :], u[at, :], h[at, :]
        sig = jax.nn.sigmoid(gate)
        act = gate * sig
        hid[at, :] = (act * up).astype(BF16)
        gate_grad = (grad * up * sig * (1.0 + gate * (1.0 - sig))).astype(BF16)
        up_grad = (grad * act).astype(BF16)
        for ref in (out, sent):
            ref[at, 0:HID] = gate_grad
            ref[at, HID : 2 * HID] = up_grad

    three = (out[0:ROWS, 0:HID], out[0:ROWS, HID : 2 * HID], hid[...])
    for i, (val, fac) in enumerate(zip(three, (gof, uof, dif))):
        at = slice(i * RANK, (i + 1) * RANK)
        ranks_out[at, :] = dot_nt(fac[...], val)
        grads[at, :] = SCALE * dot_nn(ranks[at], val)
    sent[ROWS : ROWS + RANKS, 0:HID] = ranks_out[...].astype(BF16)
    sent[ROWS : ROWS + RANKS, HID : 2 * HID] = jnp.zeros((RANKS, HID), BF16)


def run_mid(block, idx, pieces, weights, accs, factors):
    args = [idx, *pieces, *map(keep, weights), *accs, *factors]
    return pl.pallas_call(
        functools.partial(mid_kernel, block),
        out_shape=[
            shape(ROWS, 2 * HID, BF16),
            shape(ROWS + RANKS, 2 * HID, BF16),
            shape(RANKS, ROWS, F32),
            shape(RANKS, HID, F32),
        ],
        in_specs=[SM] + [VM] * (len(args) - 1),
        out_specs=[VM] * 4,
        scratch_shapes=[
            pltpu.VMEM((ROWS, HID), F32),
            pltpu.VMEM((ROWS, HID), F32),
            pltpu.VMEM((ROWS, HID), F32),
            pltpu.VMEM((RANKS, ROWS), F32),
            pltpu.VMEM((ROWS, HID), BF16),
            pltpu.VMEM((PIECE, FEATS), BF16),
        ],
        compiler_params=params(),
        cost_estimate=COST,
    )(*args)


def out_kernel(blocks, own, other, added, idx, *refs):
    refs = list(refs)
    wides = [refs.pop(0) for _ in range(own + other)]
    mine, theirs = refs[: 2 * own], refs[2 * own : 2 * own + other]
    refs = refs[2 * own + other :]
    before, outs = refs[: len(blocks)], refs[-len(blocks) :]
    for s, b in enumerate(blocks):
        terms = []
        if own:
            at = pl.ds(feature_at(idx, b), FEATS)
            terms += [(wides[0], w[at, :]) for w in mine]
        if other:
            at = 2 * BLOCKS.index(b) * FEATS
            terms += [(wides[-1], theirs[0][at + i * FEATS : at + (i + 1) * FEATS, :]) for i in range(2)]
        total = before[s][...] if added else None
        for i, (wide, w) in enumerate(terms):
            i = i % 2
            term = dot_nt(wide[0:ROWS, i * HID : (i + 1) * HID], w)
            total = term if total is None else total + term
        outs[s][...] = total.astype(outs[s].dtype)


def run_out(blocks, idx, wide, their, own_weights, their_weights, before, dtype):
    own, other, added = wide is not None, their is not None, before is not None
    args = [idx] + [wide] * own + [their] * other
    args += [keep(w) for w in (own_weights or ()) + ((their_weights,) if other else ())] + list(before or ())
    return pl.pallas_call(
        functools.partial(out_kernel, blocks, int(own), int(other), added),
        out_shape=[shape(ROWS, FEATS, dtype)] * len(blocks),
        in_specs=[SM] + [VM] * (len(args) - 1),
        out_specs=[VM] * len(blocks),
        compiler_params=params(),
        cost_estimate=COST,
    )(*args)


def first_kernel(idx, their, weights, ranks_out, p0, p1, near, far, ranks):
    for s, (p, out) in enumerate(((p0, near), (p1, far))):
        total = p[...]
        for i in range(2):
            at = (2 * s + i) * FEATS
            total = total + dot_nt(their[0:ROWS, i * HID : (i + 1) * HID], weights[at : at + FEATS, :])
        out[0:ROWS, :] = total.astype(BF16)
    for i in range(2):
        lanes, rows = slice(i * HALF, (i + 1) * HALF), slice(i * RANKS, (i + 1) * RANKS)
        chip = ranks_out[:, lanes] + their[ROWS : ROWS + RANKS, lanes].astype(F32)
        ranks[rows, :] = jnp.where(idx[2] == 0, chip, 0.0)
        near[ROWS + i * RANKS : ROWS + (i + 1) * RANKS, :] = chip.astype(BF16)


def first_out(idx, their, weights, ranks_out, parts):
    return pl.pallas_call(
        first_kernel,
        out_shape=[shape(ROWS + RIDERS, FEATS, BF16), shape(ROWS, FEATS, BF16), shape(RIDERS, FEATS, F32)],
        in_specs=[SM] + [VM] * 5,
        out_specs=[VM] * 3,
        compiler_params=params(),
        cost_estimate=COST,
    )(idx, their, keep(weights), ranks_out, *parts)


def ride_kernel(moving, here, ranks, out, ranks_now):
    out[0:ROWS, :] = (moving[0:ROWS, :].astype(F32) + here[...]).astype(BF16)
    riders = moving[ROWS : ROWS + RIDERS, :]
    out[ROWS : ROWS + RIDERS, :] = riders
    ranks_now[...] = ranks[...] + riders.astype(F32)


def ride(moving, here, ranks):
    return pl.pallas_call(
        ride_kernel,
        out_shape=[shape(ROWS + RIDERS, FEATS, BF16), shape(RIDERS, FEATS, F32)],
        in_specs=[VM] * 3,
        out_specs=[VM] * 2,
        compiler_params=params(),
        cost_estimate=COST,
    )(moving, here, ranks)


def finish_kernel(idx, mine, theirs, a0, b0, grads, adapter, ranks):
    for i in range(2):
        rows = slice(i * RANKS, (i + 1) * RANKS)
        ranks[:, i * HALF : (i + 1) * HALF] = (mine[rows, :] + theirs[rows, :].astype(F32)).astype(BF16)
    lanes = pl.ds(pl.multiple_of(idx[2] * LANES, LANES), LANES)
    for i, piece in enumerate((a0, b0)):
        at = i * RANKS
        grads[at : at + 2 * RANK, :] = SCALE * dot_nn(ranks[0 : 2 * RANK, :], piece[0:ROWS, lanes])
        grads[at + 2 * RANK : at + RANKS, :] = SCALE * dot_nn(ranks[2 * RANK : RANKS, :], piece[ROWS : 2 * ROWS, lanes])

        @pl.when(idx[2] == i)
        def _():
            adapter[...] = SCALE * dot_tn(ranks[0 : 2 * RANK, :], piece[2 * ROWS : 2 * ROWS + 2 * RANK, :])


def finish(*args):
    return pl.pallas_call(
        finish_kernel,
        out_shape=[shape(2 * RANKS, LANES, F32), shape(ROWS, FEATS, F32)],
        in_specs=[SM] + [VM] * 4,
        out_specs=[VM] * 2,
        scratch_shapes=[pltpu.VMEM((RANKS, ROWS), BF16)],
        compiler_params=params(),
        cost_estimate=COST,
    )(*args)


def join(moving, here):
    return (moving.astype(F32) + here).astype(BF16)


def flip(v, axis, n, bits):
    return lax.ppermute(v, axis, [(i, i ^ bits) for i in range(n)])


def swap(v):
    return flip(v, "core", 2, 1)


def along(v):
    return lax.ppermute(v, ("z", "core"), [(2 * z + c, 2 * ((z + 1 - 2 * c) % ZN) + c) for z in range(ZN) for c in (0, 1)])


def after(v, done):
    return lax.optimization_barrier((v, done))[0]


def body(x, dy, wg, wu, wd, gif, gof, uif, uof, dif, dof):
    yhi, z, core = lax.axis_index("yhi"), lax.axis_index("z"), lax.axis_index("core")
    idx = jnp.stack([yhi, z, core]).astype(jnp.int32)
    first = core == 0

    own = pack(x, dy, gif, uif, dof)
    a0 = ordered(idx, own, swap(own))
    with jax.named_scope("y"):
        other = flip(after(own, a0), "yhi", 2, 1)
    with jax.named_scope("a1"):
        a1 = along(a0)
    with jax.named_scope("weights"):
        chosen = choose(idx, after(wg, a0), after(wu, a0))
        their_w = swap(chosen)
        weights = load(*(after(w, a0) for w in (wg, wu, wd)))
    other = after(other, (a1, chosen, weights))
    with jax.named_scope("swap_b0"):
        b0 = ordered(idx, other, swap(other))
    with jax.named_scope("b1"):
        b1 = along(b0)

    def acc(k, r, piece, accs):
        with jax.named_scope(f"swap_{'ab'[r]}{k}"):
            theirs = swap(piece)
        with jax.named_scope(f"acc_{'ab'[r]}{k}"):
            return run_acc(((-k, r), (k, r)), idx, (piece, theirs), weights, accs)

    with jax.named_scope("acc_0"):
        accs = run_acc(((0, 0), (0, 1)), idx, (a0, b0), weights, None)
    with jax.named_scope("a2"):
        a2 = along(a1)
    with jax.named_scope("b2"):
        b2 = along(after(b1, accs[3]))
    accs = acc(1, 0, a1, accs)
    with jax.named_scope("a3"):
        a3 = along(after(a2, accs[3]))
    accs = acc(1, 1, b1, accs)
    with jax.named_scope("b3"):
        b3 = along(b2)
    accs = acc(2, 0, a2, accs)
    a3_late = after(a3, accs[3])
    accs = acc(2, 1, b2, accs)
    with jax.named_scope("a4"):
        a4_half = half_of(idx, a3)
        a4 = along(a4_half)
    with jax.named_scope("b4"):
        b4 = along(half_of(idx, b3))
    b3_late = after(b3, (accs[3], a4_half))
    accs = acc(3, 0, a3_late, accs)
    accs = acc(3, 1, b3_late, accs)
    with jax.named_scope("swap_a4"):
        a4 = (a4, swap(after(a4, accs[3])))
    with jax.named_scope("acc_a4"):
        accs = run_part((4, 0), idx, a4, weights, accs)
    with jax.named_scope("swap_b4"):
        b4 = (b4, swap(b4))
    with jax.named_scope("mid"):
        wide, sent, ranks_out, grads = run_mid((4, 1), idx, b4, weights, accs, (gof, uof, dif))
    their = swap(sent)
    mine_w = tuple(weights[0:2])
    k1, k2, k3, k4 = (BLOCKS[i : i + 2] for i in range(0, 8, 2))
    with jax.named_scope("own_part"):
        part = run_out(k1 + k2, idx, wide, None, mine_w, None, None, F32)
    with jax.named_scope("out_1"):
        n4, f3, ranks = first_out(idx, their, their_w, ranks_out, part[0:2])
    with jax.named_scope("n1"):
        near = along(n4)
    with jax.named_scope("f1"):
        far = along(f3)
    with jax.named_scope("out_2"):
        n3, f2 = run_out(k2, idx, None, their, None, their_w, part[2:4], F32)
    with jax.named_scope("out_3"):
        n2, f1 = run_out(k3, idx, wide, their, mine_w, their_w, None, F32)
    with jax.named_scope("out_4"):
        n1, n0 = run_out(k4, idx, wide, their, mine_w, their_w, None, F32)

    def hop(name, v):
        with jax.named_scope(name):
            return along(v)

    def total_rows(name, v, axis, n, bits):
        with jax.named_scope(name):
            return v + flip(v, axis, n, bits)

    def sum_x(name, v, sent):
        with jax.named_scope(name):
            other = [flip(sent, "x", 4, bits) for bits in (1, 2, 3)]
            return (v + other[0]) + (other[1] + other[2])

    near, ranks = ride(near, after(n3, f1), ranks)
    far = join(far, f2)
    near, far = hop("n2", near), hop("f2", far)
    near, ranks = ride(near, after(n2, n0), ranks)
    far = join(far, f1)
    near, far = hop("n3", near), hop("f3", far)
    near, ranks = ride(near, n1, ranks)
    near = hop("n4", near)
    grads = sum_x("out_x", grads, grads)
    ranks = ranks + jnp.where(first, near[ROWS:].astype(F32), 0.0)
    with jax.named_scope("far_core"):
        far = swap(far)
    with jax.named_scope("ranks_core"):
        by_core = swap(after(ranks.astype(BF16), (far, grads)))
    grads = total_rows("out_y", grads, "ylo", 2, 1)
    with jax.named_scope("in_grads"):
        in_grads, adapter = finish(idx, ranks, by_core, a0, b0)
    in_grads = sum_x("in_x", in_grads, in_grads)

    total = n0 + near[0:ROWS].astype(F32) + far.astype(F32) + adapter
    low, high = total[:, 0:LANES], total[:, LANES:FEATS]
    cross = [(0, 1), (1, 2), (2, 3), (3, 0)]
    with jax.named_scope("got"):
        got = lax.ppermute(jnp.where(first, high, low).astype(BF16), ("yhi", "core"), cross)
        more = lax.ppermute(high.astype(BF16), ("yhi", "core"), [(1, 3), (3, 1), (0, 0), (2, 2)])
    rows_grad = got.astype(F32) + jnp.where(first, low, more.astype(F32))
    with jax.named_scope("in_y"):
        here, there = after(in_grads[0:RANKS], (grads, got, more)), in_grads[RANKS:]
        in_grads = (here + flip(here, "ylo", 2, 1)) + (
            flip(there, "yhi", 2, 1) + flip(there, ("ylo", "yhi"), 4, 3)
        )
    g = [in_grads[i * RANK : (i + 1) * RANK] for i in range(3)]
    o = [grads[i * RANK : (i + 1) * RANK] for i in range(3)]
    return rows_grad.astype(BF16), g[0], o[0], g[1], o[1], o[2], g[2]


def solution(mesh):
    split = Mesh(mesh.devices.reshape(2, 4, 2, 8, 2), ("ylo", "x", "yhi", "z", "core"))
    dp, tensor = ("ylo", "x"), ("yhi", "z", "core")
    cols = P(None, tensor)
    return jax.shard_map(
        body,
        mesh=split,
        in_specs=(P(dp, tensor), P(dp, tensor), cols, cols, P(tensor, None), cols, cols, cols, cols, cols, cols),
        out_specs=(P(dp, tensor), cols, cols, cols, cols, cols, cols),
        check_vma=False,
    )
```

```python
import functools

import jax
import jax.numpy as jnp
from jax import lax
from jax.experimental import pallas as pl
from jax.experimental.pallas import tpu as pltpu
from jax.sharding import Mesh, PartitionSpec as P

SCALE = 0.5
ROWS = 512
HALF = ROWS // 2
LANES = 128
FEATS = 2 * LANES
HID = 512
RANK = 32
RANKS = 3 * RANK
PIECE = 2 * ROWS + RANKS
PART = PIECE // 2
RIDERS = 2 * RANKS
ZN = 8
VMEM_LIMIT = 8 * 1024 * 1024
F32 = jnp.float32
BF16 = jnp.bfloat16

VM = pl.BlockSpec(memory_space=pltpu.VMEM)
COST = pl.CostEstimate(flops=1, bytes_accessed=1, transcendentals=0)
ACC_COST = COST
PART_COST = pl.CostEstimate(flops=8 * 10**9, bytes_accessed=1, transcendentals=0)


def dot_nn(a, b):
    return lax.dot_general(a, b, (((1,), (0,)), ((), ())), preferred_element_type=F32)


def dot_nt(a, b):
    return lax.dot_general(a, b, (((1,), (1,)), ((), ())), preferred_element_type=F32)


def dot_tn(a, b):
    return lax.dot_general(a, b, (((0,), (0,)), ((), ())), preferred_element_type=F32)


def feature_at(idx, block):
    k, r = block
    core = idx[2]
    r = {"near": core, "far": 1 - core}.get(r, r)
    yhi = lax.rem(idx[0] + r, 2)
    z = lax.rem(idx[1] + k * (1 - 2 * core) + ZN, ZN)
    return pl.multiple_of((yhi * ZN + z) * FEATS, FEATS)


def params():
    return pltpu.CompilerParams(vmem_limit_bytes=VMEM_LIMIT)


def placed(kernel):
    def run(*refs):
        return kernel(tuple(lax.axis_index(a) for a in ("yhi", "z", "core")), *refs)

    return run


def keep(v):
    return pltpu.with_memory_space_constraint(v, pltpu.VMEM)


def stay(v):
    return pltpu.with_memory_space_constraint(v, pltpu.HBM)


def shape(rows, cols, dtype):
    return jax.ShapeDtypeStruct((rows, cols), dtype)


def pack_kernel(x, dy, gif, uif, dof, out, sem):
    at, copies = 0, []
    for i, ref in enumerate((x, dy, gif, uif, dof)):
        rows = ref.shape[0]
        copies.append(pltpu.make_async_copy(ref, out.at[at : at + rows, :], sem.at[i]))
        at += rows
    for c in copies:
        c.start()
    for c in copies:
        c.wait()


def pack(*arrays):
    return pl.pallas_call(
        pack_kernel,
        out_shape=shape(PIECE, LANES, BF16),
        in_specs=[pl.BlockSpec(memory_space=pl.ANY)] * 5,
        out_specs=VM,
        scratch_shapes=[pltpu.SemaphoreType.DMA((5,))],
        compiler_params=params(),
        cost_estimate=COST,
    )(*map(stay, arrays))


def load_kernel(*refs):
    n = len(refs) // 2
    ins, outs, sem = refs[:n], refs[n : 2 * n], refs[2 * n]
    copies = [pltpu.make_async_copy(a, b, sem.at[i]) for i, (a, b) in enumerate(zip(ins, outs))]
    for c in copies:
        c.start()
    for c in copies:
        c.wait()


def load(*arrays):
    return pl.pallas_call(
        load_kernel,
        out_shape=[jax.ShapeDtypeStruct(a.shape, a.dtype) for a in arrays],
        in_specs=[pl.BlockSpec(memory_space=pl.ANY)] * len(arrays),
        out_specs=[VM] * len(arrays),
        scratch_shapes=[pltpu.SemaphoreType.DMA((len(arrays),))],
        compiler_params=params(),
        cost_estimate=COST,
    )(*map(stay, arrays))


BLOCKS = ((4, "near"), (3, "far"), (3, "near"), (2, "far"), (2, "near"), (1, "far"), (1, "near"), (0, "near"))


def choose_kernel(idx, wg, wu, out, sem):
    other = (idx[0], idx[1], 1 - idx[2])
    copies = []
    for s, b in enumerate(BLOCKS):
        at = pl.ds(feature_at(other, b), FEATS)
        for i, w in enumerate((wg, wu)):
            to = out.at[pl.ds((2 * s + i) * FEATS, FEATS), :]
            copies.append(pltpu.make_async_copy(w.at[at, :], to, sem.at[s, i]))
    for c in copies:
        c.start()
    for c in copies:
        c.wait()


def choose(wg, wu):
    return pl.pallas_call(
        placed(choose_kernel),
        out_shape=shape(2 * len(BLOCKS) * FEATS, HID, BF16),
        in_specs=[pl.BlockSpec(memory_space=pl.ANY)] * 2,
        out_specs=VM,
        scratch_shapes=[pltpu.SemaphoreType.DMA((len(BLOCKS), 2))],
        compiler_params=params(),
        cost_estimate=COST,
    )(stay(wg), stay(wu))


def ordered_kernel(idx, mine, theirs, out):
    @pl.when(idx[2] == 0)
    def _():
        out[:, 0:LANES] = mine[...]
        out[:, LANES:FEATS] = theirs[...]

    @pl.when(idx[2] != 0)
    def _():
        out[:, 0:LANES] = theirs[...]
        out[:, LANES:FEATS] = mine[...]


def ordered(mine, theirs):
    return pl.pallas_call(
        placed(ordered_kernel),
        out_shape=shape(PIECE, FEATS, BF16),
        in_specs=[VM, VM],
        out_specs=VM,
        compiler_params=params(),
        cost_estimate=COST,
    )(mine, theirs)


def accumulate(blocks, first, idx, pieces, weights, accs, outs):
    wg, wu, wd = weights
    at = [feature_at(idx, b) for b in blocks]
    x, c, f = (
        jnp.concatenate([p[lo:hi, :] for p in pieces], axis=1)
        for lo, hi in ((0, ROWS), (ROWS, 2 * ROWS), (2 * ROWS, PIECE))
    )

    def put(i, sl, val):
        outs[i][sl] = val if first else accs[i][sl] + val

    put(0, Ellipsis, dot_nn(x, jnp.concatenate([wg[pl.ds(a, FEATS), :] for a in at], axis=0)))
    put(1, Ellipsis, dot_nn(x, jnp.concatenate([wu[pl.ds(a, FEATS), :] for a in at], axis=0)))
    put(2, Ellipsis, dot_nt(c, jnp.concatenate([wd[:, pl.ds(a, FEATS)] for a in at], axis=1)))
    put(3, (slice(0, 2 * RANK), slice(None)), dot_nt(f[0 : 2 * RANK], x))
    put(3, (slice(2 * RANK, RANKS), slice(None)), dot_nt(f[2 * RANK : RANKS], c))


def acc_kernel(blocks, first, idx, p0, p1, wg, wu, wd, *refs):
    accs, outs = (None, refs) if first else (refs[:4], refs[4:])
    accumulate(blocks, first, idx, (p0, p1), (wg, wu, wd), accs, outs)


ACC_SHAPES = [shape(ROWS, HID, F32)] * 3 + [shape(RANKS, ROWS, F32)]


def run_acc(blocks, pieces, weights, accs):
    first = accs is None
    args = [*pieces, *map(keep, weights)] + ([] if first else list(accs))
    aliases = {} if first else {len(args) - 4 + i: i for i in range(4)}
    return pl.pallas_call(
        placed(functools.partial(acc_kernel, blocks, first)),
        out_shape=ACC_SHAPES,
        in_specs=[VM] * len(args),
        out_specs=[VM] * 4,
        input_output_aliases=aliases,
        compiler_params=params(),
        cost_estimate=ACC_COST,
    )(*args)


def joined(idx, mine, theirs, whole):
    at = pl.multiple_of(idx[2] * PART, PART)
    whole[pl.ds(at, PART), :] = mine[...]
    whole[pl.ds(PART - at, PART), :] = theirs[...]
    return whole


def part_kernel(block, idx, mine, theirs, wg, wu, wd, *refs):
    accs, outs, whole = refs[:4], refs[4:8], refs[8]
    accumulate((block,), False, idx, (joined(idx, mine, theirs, whole),), (wg, wu, wd), accs, outs)


def run_part(block, pieces, weights, accs):
    args = [*pieces, *map(keep, weights), *accs]
    return pl.pallas_call(
        placed(functools.partial(part_kernel, block)),
        out_shape=ACC_SHAPES,
        in_specs=[VM] * len(args),
        out_specs=[VM] * 4,
        scratch_shapes=[pltpu.VMEM((PIECE, FEATS), BF16)],
        input_output_aliases={len(args) - 4 + i: i for i in range(4)},
        compiler_params=params(),
        cost_estimate=PART_COST,
    )(*args)


def half_kernel(idx, piece, out):
    out[...] = piece[pl.ds(pl.multiple_of(idx[2] * PART, PART), PART), :]


def half_of(piece):
    return pl.pallas_call(
        placed(half_kernel),
        out_shape=shape(PART, FEATS, BF16),
        in_specs=[VM],
        out_specs=VM,
        compiler_params=params(),
        cost_estimate=COST,
    )(piece)


def mid_kernel(block, idx, mine, theirs, wg, wu, wd, *refs):
    accs, (gof, uof, dif), (out, sent, ranks_out, hid, ranks_in), (g, u, h, rt, whole) = (
        refs[:4],
        refs[4:7],
        refs[7:12],
        refs[12:17],
    )
    accumulate((block,), False, idx, (joined(idx, mine, theirs, whole),), (wg, wu, wd), accs, (g, u, h, rt))
    ranks = rt[...].astype(BF16)
    ranks_in[...] = ranks
    for i, (ref, fac) in enumerate(((g, gof), (u, uof), (h, dif))):
        ref[...] += SCALE * dot_tn(ranks[i * RANK : (i + 1) * RANK], fac[...])
    step = 64

    @pl.loop(0, ROWS // step)
    def _(i):
        at = pl.ds(pl.multiple_of(i * step, step), step)
        gate, up, grad = g[at, :], u[at, :], h[at, :]
        sig = jax.nn.sigmoid(gate)
        act = gate * sig
        hid[at, :] = (act * up).astype(BF16)
        gate_grad = (grad * up * sig * (1.0 + gate * (1.0 - sig))).astype(BF16)
        up_grad = (grad * act).astype(BF16)
        for ref in (out, sent):
            ref[at, 0:HID] = gate_grad
            ref[at, HID : 2 * HID] = up_grad

    three = (out[0:ROWS, 0:HID], out[0:ROWS, HID : 2 * HID], hid[...])
    for i, (val, fac) in enumerate(zip(three, (gof, uof, dif))):
        at = slice(i * RANK, (i + 1) * RANK)
        ranks_out[at, :] = dot_nt(fac[...], val)
    sent[ROWS : ROWS + RANKS, 0:HID] = ranks_out[...].astype(BF16)
    sent[ROWS : ROWS + RANKS, HID : 2 * HID] = jnp.zeros((RANKS, HID), BF16)


def run_mid(block, pieces, weights, accs, factors):
    args = [*pieces, *map(keep, weights), *accs, *factors]
    return pl.pallas_call(
        placed(functools.partial(mid_kernel, block)),
        out_shape=[
            shape(ROWS, 2 * HID, BF16),
            shape(ROWS + RANKS, 2 * HID, BF16),
            shape(RANKS, ROWS, F32),
            shape(ROWS, HID, BF16),
            shape(RANKS, ROWS, BF16),
        ],
        in_specs=[VM] * len(args),
        out_specs=[VM] * 5,
        scratch_shapes=[
            pltpu.VMEM((ROWS, HID), F32),
            pltpu.VMEM((ROWS, HID), F32),
            pltpu.VMEM((ROWS, HID), F32),
            pltpu.VMEM((RANKS, ROWS), F32),
            pltpu.VMEM((PIECE, FEATS), BF16),
        ],
        compiler_params=params(),
        cost_estimate=COST,
    )(*args)


def factor_kernel(wide, hid, ranks, grads):
    for i, val in enumerate((wide[:, 0:HID], wide[:, HID : 2 * HID], hid[...])):
        at = slice(i * RANK, (i + 1) * RANK)
        grads[at, :] = SCALE * dot_nn(ranks[at, :], val)


def factor_grads(*args):
    return pl.pallas_call(
        factor_kernel,
        out_shape=shape(RANKS, HID, F32),
        in_specs=[VM] * 3,
        out_specs=VM,
        compiler_params=params(),
        cost_estimate=COST,
    )(*args)


def out_kernel(blocks, own, other, added, idx, *refs):
    refs = list(refs)
    wides = [refs.pop(0) for _ in range(own + other)]
    mine, theirs = refs[: 2 * own], refs[2 * own : 2 * own + other]
    refs = refs[2 * own + other :]
    before, outs = refs[: len(blocks)], refs[-len(blocks) :]
    for s, b in enumerate(blocks):
        terms = []
        if own:
            at = pl.ds(feature_at(idx, b), FEATS)
            terms += [(wides[0], w[at, :]) for w in mine]
        if other:
            at = 2 * BLOCKS.index(b) * FEATS
            terms += [(wides[-1], theirs[0][at + i * FEATS : at + (i + 1) * FEATS, :]) for i in range(2)]
        total = before[s][...] if added else None
        for i, (wide, w) in enumerate(terms):
            i = i % 2
            term = dot_nt(wide[0:ROWS, i * HID : (i + 1) * HID], w)
            total = term if total is None else total + term
        outs[s][...] = total.astype(outs[s].dtype)


def run_out(blocks, wide, their, own_weights, their_weights, before, dtype):
    own, other, added = wide is not None, their is not None, before is not None
    args = [wide] * own + [their] * other
    args += [keep(w) for w in (own_weights or ()) + ((their_weights,) if other else ())] + list(before or ())
    return pl.pallas_call(
        placed(functools.partial(out_kernel, blocks, int(own), int(other), added)),
        out_shape=[shape(ROWS, FEATS, dtype)] * len(blocks),
        in_specs=[VM] * len(args),
        out_specs=[VM] * len(blocks),
        compiler_params=params(),
        cost_estimate=COST,
    )(*args)


def first_kernel(idx, their, weights, ranks_out, p0, p1, near, far, ranks):
    for s, (p, out) in enumerate(((p0, near), (p1, far))):
        total = p[...]
        for i in range(2):
            at = (2 * s + i) * FEATS
            total = total + dot_nt(their[0:ROWS, i * HID : (i + 1) * HID], weights[at : at + FEATS, :])
        out[0:ROWS, :] = total.astype(BF16)
    for i in range(2):
        lanes, rows = slice(i * HALF, (i + 1) * HALF), slice(i * RANKS, (i + 1) * RANKS)
        chip = ranks_out[:, lanes] + their[ROWS : ROWS + RANKS, lanes].astype(F32)
        ranks[rows, :] = jnp.where(idx[2] == 0, chip, 0.0)
        near[ROWS + i * RANKS : ROWS + (i + 1) * RANKS, :] = chip.astype(BF16)


def first_out(their, weights, ranks_out, parts):
    return pl.pallas_call(
        placed(first_kernel),
        out_shape=[shape(ROWS + RIDERS, FEATS, BF16), shape(ROWS, FEATS, BF16), shape(RIDERS, FEATS, F32)],
        in_specs=[VM] * 5,
        out_specs=[VM] * 3,
        compiler_params=params(),
        cost_estimate=COST,
    )(their, keep(weights), ranks_out, *parts)


def ride_kernel(moving, here, ranks, out, ranks_now):
    out[0:ROWS, :] = (moving[0:ROWS, :].astype(F32) + here[...]).astype(BF16)
    riders = moving[ROWS : ROWS + RIDERS, :]
    out[ROWS : ROWS + RIDERS, :] = riders
    ranks_now[...] = ranks[...] + riders.astype(F32)


def ride(moving, here, ranks):
    return pl.pallas_call(
        ride_kernel,
        out_shape=[shape(ROWS + RIDERS, FEATS, BF16), shape(RIDERS, FEATS, F32)],
        in_specs=[VM] * 3,
        out_specs=[VM] * 2,
        compiler_params=params(),
        cost_estimate=COST,
    )(moving, here, ranks)


def finish_kernel(idx, mine, theirs, a0, b0, grads, adapter, ranks):
    for i in range(2):
        rows = slice(i * RANKS, (i + 1) * RANKS)
        ranks[:, i * HALF : (i + 1) * HALF] = (mine[rows, :] + theirs[rows, :].astype(F32)).astype(BF16)
    lanes = pl.ds(pl.multiple_of(idx[2] * LANES, LANES), LANES)
    for i, piece in enumerate((a0, b0)):
        at = i * RANKS
        grads[at : at + 2 * RANK, :] = SCALE * dot_nn(ranks[0 : 2 * RANK, :], piece[0:ROWS, lanes])
        grads[at + 2 * RANK : at + RANKS, :] = SCALE * dot_nn(ranks[2 * RANK : RANKS, :], piece[ROWS : 2 * ROWS, lanes])

        @pl.when(idx[2] == i)
        def _():
            adapter[...] = SCALE * dot_tn(ranks[0 : 2 * RANK, :], piece[2 * ROWS : 2 * ROWS + 2 * RANK, :])


def finish(*args):
    return pl.pallas_call(
        placed(finish_kernel),
        out_shape=[shape(2 * RANKS, LANES, F32), shape(ROWS, FEATS, F32)],
        in_specs=[VM] * 4,
        out_specs=[VM] * 2,
        scratch_shapes=[pltpu.VMEM((RANKS, ROWS), BF16)],
        compiler_params=params(),
        cost_estimate=COST,
    )(*args)


def join(moving, here):
    return (moving.astype(F32) + here).astype(BF16)


def flip(v, axis, n, bits):
    return lax.ppermute(v, axis, [(i, i ^ bits) for i in range(n)])


def swap(v):
    return flip(v, "core", 2, 1)


def along(v):
    return lax.ppermute(v, ("z", "core"), [(2 * z + c, 2 * ((z + 1 - 2 * c) % ZN) + c) for z in range(ZN) for c in (0, 1)])


def after(v, done):
    return lax.optimization_barrier((v, done))[0]


def body(x, dy, wg, wu, wd, gif, gof, uif, uof, dif, dof):
    first = lax.axis_index("core") == 0

    own = pack(x, dy, gif, uif, dof)
    a0 = ordered(own, swap(own))
    with jax.named_scope("y"):
        other = flip(after(own, a0), "yhi", 2, 1)
    with jax.named_scope("a1"):
        a1 = along(a0)
    with jax.named_scope("weights"):
        chosen = choose(after(wg, a0), after(wu, a0))
        their_w = swap(chosen)
        weights = load(*(after(w, a0) for w in (wg, wu, wd)))
    other = after(other, (a1, chosen, weights))
    with jax.named_scope("swap_b0"):
        b0 = ordered(other, swap(other))
    with jax.named_scope("b1"):
        b1 = along(b0)

    def acc(k, r, piece, accs):
        with jax.named_scope(f"swap_{'ab'[r]}{k}"):
            theirs = swap(piece)
        with jax.named_scope(f"acc_{'ab'[r]}{k}"):
            return run_acc(((-k, r), (k, r)), (piece, theirs), weights, accs)

    with jax.named_scope("acc_0"):
        accs = run_acc(((0, 0), (0, 1)), (a0, b0), weights, None)
    with jax.named_scope("a2"):
        a2 = along(a1)
    with jax.named_scope("b2"):
        b2 = along(after(b1, accs[3]))
    accs = acc(1, 0, a1, accs)
    with jax.named_scope("a3"):
        a3 = along(after(a2, accs[3]))
    accs = acc(1, 1, b1, accs)
    with jax.named_scope("b3"):
        b3 = along(b2)
    accs = acc(2, 0, a2, accs)
    a3_late = after(a3, accs[3])
    accs = acc(2, 1, b2, accs)
    with jax.named_scope("a4"):
        a4_half = half_of(a3)
        a4 = along(a4_half)
    with jax.named_scope("b4"):
        b4 = along(half_of(b3))
    b3_late = after(b3, (accs[3], a4_half))
    accs = acc(3, 0, a3_late, accs)
    accs = acc(3, 1, b3_late, accs)
    with jax.named_scope("swap_a4"):
        a4 = (a4, swap(after(a4, accs[3])))
    with jax.named_scope("acc_a4"):
        accs = run_part((4, 0), a4, weights, accs)
    with jax.named_scope("swap_b4"):
        b4 = (b4, swap(b4))
    with jax.named_scope("mid"):
        wide, sent, ranks_out, hid, ranks_in = run_mid((4, 1), b4, weights, accs, (gof, uof, dif))
    their = swap(sent)
    mine_w = tuple(weights[0:2])
    k1, k2, k3, k4 = (BLOCKS[i : i + 2] for i in range(0, 8, 2))
    with jax.named_scope("own_part"):
        part = run_out(k1 + k2, wide, None, mine_w, None, None, F32)
    with jax.named_scope("out_1"):
        n4, f3, ranks = first_out(their, their_w, ranks_out, part[0:2])
    with jax.named_scope("n1"):
        near = along(n4)
    with jax.named_scope("f1"):
        far = along(f3)
    with jax.named_scope("out_2"):
        n3, f2 = run_out(k2, None, their, None, their_w, part[2:4], F32)
    with jax.named_scope("out_3"):
        n2, f1 = run_out(k3, wide, their, mine_w, their_w, None, F32)
    with jax.named_scope("out_4"):
        n1, n0 = run_out(k4, wide, their, mine_w, their_w, None, F32)

    def hop(name, v):
        with jax.named_scope(name):
            return along(v)

    def total_rows(name, v, axis, n, bits):
        with jax.named_scope(name):
            return v + flip(v, axis, n, bits)

    def sum_x(name, v, sent):
        with jax.named_scope(name):
            other = [flip(sent, "x", 4, bits) for bits in (1, 2, 3)]
            return (v + other[0]) + (other[1] + other[2])

    with jax.named_scope("factor_grads"):
        grads = factor_grads(wide, hid, ranks_in)
    near, ranks = ride(near, after(n3, f1), ranks)
    far = join(far, f2)
    near, far = hop("n2", near), hop("f2", far)
    near, ranks = ride(near, after(n2, n0), ranks)
    far = join(far, f1)
    near, far = hop("n3", near), hop("f3", far)
    near, ranks = ride(near, n1, ranks)
    near = hop("n4", near)
    grads = sum_x("out_x", grads, grads)
    ranks = ranks + jnp.where(first, near[ROWS:].astype(F32), 0.0)
    with jax.named_scope("far_core"):
        far = swap(far)
    with jax.named_scope("ranks_core"):
        by_core = swap(after(ranks.astype(BF16), (far, grads)))
    grads = total_rows("out_y", after(grads, by_core), "ylo", 2, 1)
    with jax.named_scope("in_grads"):
        in_grads, adapter = finish(ranks, by_core, a0, b0)
    in_grads = sum_x("in_x", in_grads, in_grads)

    total = n0 + near[0:ROWS].astype(F32) + far.astype(F32) + adapter
    low, high = total[:, 0:LANES], total[:, LANES:FEATS]
    cross = [(0, 1), (1, 2), (2, 3), (3, 0)]
    with jax.named_scope("got"):
        got = lax.ppermute(jnp.where(first, high, low).astype(BF16), ("yhi", "core"), cross)
        more = lax.ppermute(high.astype(BF16), ("yhi", "core"), [(1, 3), (3, 1), (0, 0), (2, 2)])
    rows_grad = got.astype(F32) + jnp.where(first, low, more.astype(F32))
    with jax.named_scope("in_y"):
        here, there = after(in_grads[0:RANKS], (grads, got, more)), in_grads[RANKS:]
        in_grads = (here + flip(here, "ylo", 2, 1)) + (
            flip(there, "yhi", 2, 1) + flip(there, ("ylo", "yhi"), 4, 3)
        )
    g = [in_grads[i * RANK : (i + 1) * RANK] for i in range(3)]
    o = [grads[i * RANK : (i + 1) * RANK] for i in range(3)]
    return rows_grad.astype(BF16), g[0], o[0], g[1], o[1], o[2], g[2]


def solution(mesh):
    split = Mesh(mesh.devices.reshape(2, 4, 2, 8, 2), ("ylo", "x", "yhi", "z", "core"))
    dp, tensor = ("ylo", "x"), ("yhi", "z", "core")
    cols = P(None, tensor)
    return jax.shard_map(
        body,
        mesh=split,
        in_specs=(P(dp, tensor), P(dp, tensor), cols, cols, P(tensor, None), cols, cols, cols, cols, cols, cols),
        out_specs=(P(dp, tensor), cols, cols, cols, cols, cols, cols),
        check_vma=False,
    )
```

```python
import functools

import jax
import jax.numpy as jnp
from jax import lax
from jax.experimental import pallas as pl
from jax.experimental.pallas import tpu as pltpu
from jax.sharding import Mesh, PartitionSpec as P

SCALE = 0.5
ROWS = 512
HALF = ROWS // 2
LANES = 128
FEATS = 2 * LANES
HID = 512
RANK = 32
RANKS = 3 * RANK
PIECE = 2 * ROWS + RANKS
PART = PIECE // 2
RIDERS = 2 * RANKS
FOLDED = RANKS // 2
ZN = 8
VMEM_LIMIT = 8 * 1024 * 1024
F32 = jnp.float32
BF16 = jnp.bfloat16

VM = pl.BlockSpec(memory_space=pltpu.VMEM)
COST = pl.CostEstimate(flops=1, bytes_accessed=1, transcendentals=0)
ACC_COST = COST
PART_COST = pl.CostEstimate(flops=8 * 10**9, bytes_accessed=1, transcendentals=0)


def dot_nn(a, b):
    return lax.dot_general(a, b, (((1,), (0,)), ((), ())), preferred_element_type=F32)


def dot_nt(a, b):
    return lax.dot_general(a, b, (((1,), (1,)), ((), ())), preferred_element_type=F32)


def dot_tn(a, b):
    return lax.dot_general(a, b, (((0,), (0,)), ((), ())), preferred_element_type=F32)


def feature_at(idx, block):
    k, r = block
    core = idx[2]
    r = {"near": core, "far": 1 - core}.get(r, r)
    yhi = lax.rem(idx[0] + r, 2)
    z = lax.rem(idx[1] + k * (1 - 2 * core) + ZN, ZN)
    return pl.multiple_of((yhi * ZN + z) * FEATS, FEATS)


def params():
    return pltpu.CompilerParams(vmem_limit_bytes=VMEM_LIMIT)


def placed(kernel):
    def run(*refs):
        return kernel(tuple(lax.axis_index(a) for a in ("yhi", "z", "core")), *refs)

    return run


def keep(v):
    return pltpu.with_memory_space_constraint(v, pltpu.VMEM)


def stay(v):
    return pltpu.with_memory_space_constraint(v, pltpu.HBM)


def shape(rows, cols, dtype):
    return jax.ShapeDtypeStruct((rows, cols), dtype)


def pack_kernel(x, dy, gif, uif, dof, out, sem):
    at, copies = 0, []
    for i, ref in enumerate((x, dy, gif, uif, dof)):
        rows = ref.shape[0]
        copies.append(pltpu.make_async_copy(ref, out.at[at : at + rows, :], sem.at[i]))
        at += rows
    for c in copies:
        c.start()
    for c in copies:
        c.wait()


def pack(*arrays):
    return pl.pallas_call(
        pack_kernel,
        out_shape=shape(PIECE, LANES, BF16),
        in_specs=[pl.BlockSpec(memory_space=pl.ANY)] * 5,
        out_specs=VM,
        scratch_shapes=[pltpu.SemaphoreType.DMA((5,))],
        compiler_params=params(),
        cost_estimate=COST,
    )(*map(stay, arrays))


def load_kernel(*refs):
    n = len(refs) // 2
    ins, outs, sem = refs[:n], refs[n : 2 * n], refs[2 * n]
    copies = [pltpu.make_async_copy(a, b, sem.at[i]) for i, (a, b) in enumerate(zip(ins, outs))]
    for c in copies:
        c.start()
    for c in copies:
        c.wait()


def load(*arrays):
    return pl.pallas_call(
        load_kernel,
        out_shape=[jax.ShapeDtypeStruct(a.shape, a.dtype) for a in arrays],
        in_specs=[pl.BlockSpec(memory_space=pl.ANY)] * len(arrays),
        out_specs=[VM] * len(arrays),
        scratch_shapes=[pltpu.SemaphoreType.DMA((len(arrays),))],
        compiler_params=params(),
        cost_estimate=COST,
    )(*map(stay, arrays))


BLOCKS = ((4, "near"), (3, "far"), (3, "near"), (2, "far"), (2, "near"), (1, "far"), (1, "near"), (0, "near"))


def choose_kernel(idx, wg, wu, out, sem):
    other = (idx[0], idx[1], 1 - idx[2])
    copies = []
    for s, b in enumerate(BLOCKS):
        at = pl.ds(feature_at(other, b), FEATS)
        for i, w in enumerate((wg, wu)):
            to = out.at[pl.ds((2 * s + i) * FEATS, FEATS), :]
            copies.append(pltpu.make_async_copy(w.at[at, :], to, sem.at[s, i]))
    for c in copies:
        c.start()
    for c in copies:
        c.wait()


def choose(wg, wu):
    return pl.pallas_call(
        placed(choose_kernel),
        out_shape=shape(2 * len(BLOCKS) * FEATS, HID, BF16),
        in_specs=[pl.BlockSpec(memory_space=pl.ANY)] * 2,
        out_specs=VM,
        scratch_shapes=[pltpu.SemaphoreType.DMA((len(BLOCKS), 2))],
        compiler_params=params(),
        cost_estimate=COST,
    )(stay(wg), stay(wu))


def ordered_kernel(idx, mine, theirs, out):
    @pl.when(idx[2] == 0)
    def _():
        out[:, 0:LANES] = mine[...]
        out[:, LANES:FEATS] = theirs[...]

    @pl.when(idx[2] != 0)
    def _():
        out[:, 0:LANES] = theirs[...]
        out[:, LANES:FEATS] = mine[...]


def ordered(mine, theirs):
    return pl.pallas_call(
        placed(ordered_kernel),
        out_shape=shape(PIECE, FEATS, BF16),
        in_specs=[VM, VM],
        out_specs=VM,
        compiler_params=params(),
        cost_estimate=COST,
    )(mine, theirs)


def accumulate(blocks, first, idx, pieces, weights, accs, outs):
    wg, wu, wd = weights
    at = [feature_at(idx, b) for b in blocks]
    x, c, f = (
        jnp.concatenate([p[lo:hi, :] for p in pieces], axis=1)
        for lo, hi in ((0, ROWS), (ROWS, 2 * ROWS), (2 * ROWS, PIECE))
    )

    def put(i, sl, val):
        outs[i][sl] = val if first else accs[i][sl] + val

    put(0, Ellipsis, dot_nn(x, jnp.concatenate([wg[pl.ds(a, FEATS), :] for a in at], axis=0)))
    put(1, Ellipsis, dot_nn(x, jnp.concatenate([wu[pl.ds(a, FEATS), :] for a in at], axis=0)))
    put(2, Ellipsis, dot_nt(c, jnp.concatenate([wd[:, pl.ds(a, FEATS)] for a in at], axis=1)))
    put(3, (slice(0, 2 * RANK), slice(None)), dot_nt(f[0 : 2 * RANK], x))
    put(3, (slice(2 * RANK, RANKS), slice(None)), dot_nt(f[2 * RANK : RANKS], c))


def acc_kernel(blocks, first, idx, p0, p1, wg, wu, wd, *refs):
    accs, outs = (None, refs) if first else (refs[:4], refs[4:])
    accumulate(blocks, first, idx, (p0, p1), (wg, wu, wd), accs, outs)


ACC_SHAPES = [shape(ROWS, HID, F32)] * 3 + [shape(RANKS, ROWS, F32)]


def run_acc(blocks, pieces, weights, accs):
    first = accs is None
    args = [*pieces, *map(keep, weights)] + ([] if first else list(accs))
    aliases = {} if first else {len(args) - 4 + i: i for i in range(4)}
    return pl.pallas_call(
        placed(functools.partial(acc_kernel, blocks, first)),
        out_shape=ACC_SHAPES,
        in_specs=[VM] * len(args),
        out_specs=[VM] * 4,
        input_output_aliases=aliases,
        compiler_params=params(),
        cost_estimate=ACC_COST,
    )(*args)


def joined(idx, mine, theirs, whole):
    at = pl.multiple_of(idx[2] * PART, PART)
    whole[pl.ds(at, PART), :] = mine[...]
    whole[pl.ds(PART - at, PART), :] = theirs[...]
    return whole


def part_kernel(block, idx, mine, theirs, wg, wu, wd, *refs):
    accs, outs, whole = refs[:4], refs[4:8], refs[8]
    accumulate((block,), False, idx, (joined(idx, mine, theirs, whole),), (wg, wu, wd), accs, outs)


def run_part(block, pieces, weights, accs):
    args = [*pieces, *map(keep, weights), *accs]
    return pl.pallas_call(
        placed(functools.partial(part_kernel, block)),
        out_shape=ACC_SHAPES,
        in_specs=[VM] * len(args),
        out_specs=[VM] * 4,
        scratch_shapes=[pltpu.VMEM((PIECE, FEATS), BF16)],
        input_output_aliases={len(args) - 4 + i: i for i in range(4)},
        compiler_params=params(),
        cost_estimate=PART_COST,
    )(*args)


def half_kernel(idx, piece, out):
    out[...] = piece[pl.ds(pl.multiple_of(idx[2] * PART, PART), PART), :]


def half_of(piece):
    return pl.pallas_call(
        placed(half_kernel),
        out_shape=shape(PART, FEATS, BF16),
        in_specs=[VM],
        out_specs=VM,
        compiler_params=params(),
        cost_estimate=COST,
    )(piece)


def mid_kernel(block, idx, mine, theirs, wg, wu, wd, *refs):
    accs, (gof, uof, dif), (out, sent, ranks_out, hid, ranks_in), (g, u, h, rt, whole) = (
        refs[:4],
        refs[4:7],
        refs[7:12],
        refs[12:17],
    )
    accumulate((block,), False, idx, (joined(idx, mine, theirs, whole),), (wg, wu, wd), accs, (g, u, h, rt))
    ranks = rt[...].astype(BF16)
    ranks_in[...] = ranks
    for i, (ref, fac) in enumerate(((g, gof), (u, uof), (h, dif))):
        ref[...] += SCALE * dot_tn(ranks[i * RANK : (i + 1) * RANK], fac[...])
    step = 64

    @pl.loop(0, ROWS // step)
    def _(i):
        at = pl.ds(pl.multiple_of(i * step, step), step)
        gate, up, grad = g[at, :], u[at, :], h[at, :]
        sig = jax.nn.sigmoid(gate)
        act = gate * sig
        hid[at, :] = (act * up).astype(BF16)
        gate_grad = (grad * up * sig * (1.0 + gate * (1.0 - sig))).astype(BF16)
        up_grad = (grad * act).astype(BF16)
        for ref in (out, sent):
            ref[at, 0:HID] = gate_grad
            ref[at, HID : 2 * HID] = up_grad

    three = (out[0:ROWS, 0:HID], out[0:ROWS, HID : 2 * HID], hid[...])
    for i, (val, fac) in enumerate(zip(three, (gof, uof, dif))):
        at = slice(i * RANK, (i + 1) * RANK)
        ranks_out[at, :] = dot_nt(fac[...], val)
    for i in range(2):
        rows = slice(i * FOLDED, (i + 1) * FOLDED)
        sent[ROWS : ROWS + FOLDED, i * HID : (i + 1) * HID] = ranks_out[rows, :].astype(BF16)


def run_mid(block, pieces, weights, accs, factors):
    args = [*pieces, *map(keep, weights), *accs, *factors]
    return pl.pallas_call(
        placed(functools.partial(mid_kernel, block)),
        out_shape=[
            shape(ROWS, 2 * HID, BF16),
            shape(ROWS + FOLDED, 2 * HID, BF16),
            shape(RANKS, ROWS, F32),
            shape(ROWS, HID, BF16),
            shape(RANKS, ROWS, BF16),
        ],
        in_specs=[VM] * len(args),
        out_specs=[VM] * 5,
        scratch_shapes=[
            pltpu.VMEM((ROWS, HID), F32),
            pltpu.VMEM((ROWS, HID), F32),
            pltpu.VMEM((ROWS, HID), F32),
            pltpu.VMEM((RANKS, ROWS), F32),
            pltpu.VMEM((PIECE, FEATS), BF16),
        ],
        compiler_params=params(),
        cost_estimate=COST,
    )(*args)


def factor_kernel(wide, hid, ranks, grads):
    for i, val in enumerate((wide[:, 0:HID], wide[:, HID : 2 * HID], hid[...])):
        at = slice(i * RANK, (i + 1) * RANK)
        grads[at, :] = SCALE * dot_nn(ranks[at, :], val)


def factor_grads(*args):
    return pl.pallas_call(
        factor_kernel,
        out_shape=shape(RANKS, HID, F32),
        in_specs=[VM] * 3,
        out_specs=VM,
        compiler_params=params(),
        cost_estimate=COST,
    )(*args)


def out_kernel(blocks, own, other, added, idx, *refs):
    refs = list(refs)
    wides = [refs.pop(0) for _ in range(own + other)]
    mine, theirs = refs[: 2 * own], refs[2 * own : 2 * own + other]
    refs = refs[2 * own + other :]
    before, outs = refs[: len(blocks)], refs[-len(blocks) :]
    for s, b in enumerate(blocks):
        terms = []
        if own:
            at = pl.ds(feature_at(idx, b), FEATS)
            terms += [(wides[0], w[at, :]) for w in mine]
        if other:
            at = 2 * BLOCKS.index(b) * FEATS
            terms += [(wides[-1], theirs[0][at + i * FEATS : at + (i + 1) * FEATS, :]) for i in range(2)]
        total = before[s][...] if added else None
        for i, (wide, w) in enumerate(terms):
            i = i % 2
            term = dot_nt(wide[0:ROWS, i * HID : (i + 1) * HID], w)
            total = term if total is None else total + term
        outs[s][...] = total.astype(outs[s].dtype)


def run_out(blocks, wide, their, own_weights, their_weights, before, dtype):
    own, other, added = wide is not None, their is not None, before is not None
    args = [wide] * own + [their] * other
    args += [keep(w) for w in (own_weights or ()) + ((their_weights,) if other else ())] + list(before or ())
    return pl.pallas_call(
        placed(functools.partial(out_kernel, blocks, int(own), int(other), added)),
        out_shape=[shape(ROWS, FEATS, dtype)] * len(blocks),
        in_specs=[VM] * len(args),
        out_specs=[VM] * len(blocks),
        compiler_params=params(),
        cost_estimate=COST,
    )(*args)


def first_kernel(idx, their, weights, ranks_out, p0, p1, near, far, ranks):
    for s, (p, out) in enumerate(((p0, near), (p1, far))):
        total = p[...]
        for i in range(2):
            at = (2 * s + i) * FEATS
            total = total + dot_nt(their[0:ROWS, i * HID : (i + 1) * HID], weights[at : at + FEATS, :])
        out[0:ROWS, :] = total.astype(BF16)
    for i in range(2):
        lanes, rows = slice(i * HALF, (i + 1) * HALF), slice(i * RANKS, (i + 1) * RANKS)
        folded = [their[ROWS : ROWS + FOLDED, at + i * HALF : at + (i + 1) * HALF] for at in (0, HID)]
        chip = ranks_out[:, lanes] + jnp.concatenate([v.astype(F32) for v in folded], axis=0)
        ranks[rows, :] = jnp.where(idx[2] == 0, chip, 0.0)
        near[ROWS + i * RANKS : ROWS + (i + 1) * RANKS, :] = chip.astype(BF16)


def first_out(their, weights, ranks_out, parts):
    return pl.pallas_call(
        placed(first_kernel),
        out_shape=[shape(ROWS + RIDERS, FEATS, BF16), shape(ROWS, FEATS, BF16), shape(RIDERS, FEATS, F32)],
        in_specs=[VM] * 5,
        out_specs=[VM] * 3,
        compiler_params=params(),
        cost_estimate=COST,
    )(their, keep(weights), ranks_out, *parts)


def ride_kernel(moving, here, ranks, out, ranks_now):
    out[0:ROWS, :] = (moving[0:ROWS, :].astype(F32) + here[...]).astype(BF16)
    riders = moving[ROWS : ROWS + RIDERS, :]
    out[ROWS : ROWS + RIDERS, :] = riders
    ranks_now[...] = ranks[...] + riders.astype(F32)


def ride(moving, here, ranks):
    return pl.pallas_call(
        ride_kernel,
        out_shape=[shape(ROWS + RIDERS, FEATS, BF16), shape(RIDERS, FEATS, F32)],
        in_specs=[VM] * 3,
        out_specs=[VM] * 2,
        compiler_params=params(),
        cost_estimate=COST,
    )(moving, here, ranks)


def finish_kernel(idx, mine, theirs, a0, b0, grads, adapter, ranks):
    for i in range(2):
        rows = slice(i * RANKS, (i + 1) * RANKS)
        ranks[:, i * HALF : (i + 1) * HALF] = (mine[rows, :] + theirs[rows, :].astype(F32)).astype(BF16)
    lanes = pl.ds(pl.multiple_of(idx[2] * LANES, LANES), LANES)
    for i, piece in enumerate((a0, b0)):
        at = i * RANKS
        grads[at : at + 2 * RANK, :] = SCALE * dot_nn(ranks[0 : 2 * RANK, :], piece[0:ROWS, lanes])
        grads[at + 2 * RANK : at + RANKS, :] = SCALE * dot_nn(ranks[2 * RANK : RANKS, :], piece[ROWS : 2 * ROWS, lanes])

        @pl.when(idx[2] == i)
        def _():
            adapter[...] = SCALE * dot_tn(ranks[0 : 2 * RANK, :], piece[2 * ROWS : 2 * ROWS + 2 * RANK, :])


def finish(*args):
    return pl.pallas_call(
        placed(finish_kernel),
        out_shape=[shape(2 * RANKS, LANES, F32), shape(ROWS, FEATS, F32)],
        in_specs=[VM] * 4,
        out_specs=[VM] * 2,
        scratch_shapes=[pltpu.VMEM((RANKS, ROWS), BF16)],
        compiler_params=params(),
        cost_estimate=COST,
    )(*args)


def join(moving, here):
    return (moving.astype(F32) + here).astype(BF16)


def flip(v, axis, n, bits):
    return lax.ppermute(v, axis, [(i, i ^ bits) for i in range(n)])


def swap(v):
    return flip(v, "core", 2, 1)


def along(v):
    return lax.ppermute(v, ("z", "core"), [(2 * z + c, 2 * ((z + 1 - 2 * c) % ZN) + c) for z in range(ZN) for c in (0, 1)])


def after(v, done):
    return lax.optimization_barrier((v, done))[0]


def body(x, dy, wg, wu, wd, gif, gof, uif, uof, dif, dof):
    first = lax.axis_index("core") == 0

    own = pack(x, dy, gif, uif, dof)
    a0 = ordered(own, swap(own))
    with jax.named_scope("y"):
        other = flip(after(own, a0), "yhi", 2, 1)
    with jax.named_scope("a1"):
        a1 = along(a0)
    with jax.named_scope("weights"):
        chosen = choose(after(wg, a0), after(wu, a0))
        their_w = swap(chosen)
        weights = load(*(after(w, a0) for w in (wg, wu, wd)))
    other = after(other, (a1, chosen, weights))
    with jax.named_scope("swap_b0"):
        b0 = ordered(other, swap(other))
    with jax.named_scope("b1"):
        b1 = along(b0)

    def acc(k, r, piece, accs):
        with jax.named_scope(f"swap_{'ab'[r]}{k}"):
            theirs = swap(piece)
        with jax.named_scope(f"acc_{'ab'[r]}{k}"):
            return run_acc(((-k, r), (k, r)), (piece, theirs), weights, accs)

    with jax.named_scope("acc_0"):
        accs = run_acc(((0, 0), (0, 1)), (a0, b0), weights, None)
    with jax.named_scope("a2"):
        a2 = along(a1)
    with jax.named_scope("b2"):
        b2 = along(after(b1, accs[3]))
    accs = acc(1, 0, a1, accs)
    with jax.named_scope("a3"):
        a3 = along(after(a2, accs[3]))
    accs = acc(1, 1, b1, accs)
    with jax.named_scope("b3"):
        b3 = along(b2)
    accs = acc(2, 0, a2, accs)
    a3_late = after(a3, accs[3])
    accs = acc(2, 1, b2, accs)
    with jax.named_scope("a4"):
        a4_half = half_of(a3)
        a4 = along(a4_half)
    with jax.named_scope("b4"):
        b4 = along(half_of(b3))
    b3_late = after(b3, (accs[3], a4_half))
    accs = acc(3, 0, a3_late, accs)
    accs = acc(3, 1, b3_late, accs)
    with jax.named_scope("swap_a4"):
        a4 = (a4, swap(after(a4, accs[3])))
    with jax.named_scope("acc_a4"):
        accs = run_part((4, 0), a4, weights, accs)
    with jax.named_scope("swap_b4"):
        b4 = (b4, swap(b4))
    with jax.named_scope("mid"):
        wide, sent, ranks_out, hid, ranks_in = run_mid((4, 1), b4, weights, accs, (gof, uof, dif))
    their = swap(sent)
    mine_w = tuple(weights[0:2])
    k1, k2, k3, k4 = (BLOCKS[i : i + 2] for i in range(0, 8, 2))
    with jax.named_scope("own_part"):
        part = run_out(k1 + k2, wide, None, mine_w, None, None, F32)
    with jax.named_scope("out_1"):
        n4, f3, ranks = first_out(their, their_w, ranks_out, part[0:2])
    with jax.named_scope("n1"):
        near = along(n4)
    with jax.named_scope("f1"):
        far = along(f3)
    with jax.named_scope("out_2"):
        n3, f2 = run_out(k2, None, their, None, their_w, part[2:4], F32)
    with jax.named_scope("out_3"):
        n2, f1 = run_out(k3, wide, their, mine_w, their_w, None, F32)
    with jax.named_scope("out_4"):
        n1, n0 = run_out(k4, wide, their, mine_w, their_w, None, F32)

    def hop(name, v):
        with jax.named_scope(name):
            return along(v)

    def total_rows(name, v, axis, n, bits):
        with jax.named_scope(name):
            return v + flip(v, axis, n, bits)

    def sum_x(name, v, sent):
        with jax.named_scope(name):
            other = [flip(sent, "x", 4, bits) for bits in (1, 2, 3)]
            return (v + other[0]) + (other[1] + other[2])

    with jax.named_scope("factor_grads"):
        grads = factor_grads(wide, hid, ranks_in)
    near, ranks = ride(near, after(n3, f1), ranks)
    far = join(far, f2)
    near, far = hop("n2", near), hop("f2", far)
    near, ranks = ride(near, after(n2, n0), ranks)
    far = join(far, f1)
    near, far = hop("n3", near), hop("f3", far)
    near, ranks = ride(near, n1, ranks)
    near = hop("n4", near)
    grads = sum_x("out_x", grads, grads)
    ranks = ranks + jnp.where(first, near[ROWS:].astype(F32), 0.0)
    with jax.named_scope("far_core"):
        far = swap(far)
    with jax.named_scope("ranks_core"):
        by_core = swap(after(ranks.astype(BF16), (far, grads)))
    grads = total_rows("out_y", after(grads, by_core), "ylo", 2, 1)
    with jax.named_scope("in_grads"):
        in_grads, adapter = finish(ranks, by_core, a0, b0)
    in_grads = sum_x("in_x", in_grads, in_grads)

    total = n0 + near[0:ROWS].astype(F32) + far.astype(F32) + adapter
    low, high = total[:, 0:LANES], total[:, LANES:FEATS]
    cross = [(0, 1), (1, 2), (2, 3), (3, 0)]
    with jax.named_scope("got"):
        got = lax.ppermute(jnp.where(first, high, low).astype(BF16), ("yhi", "core"), cross)
        more = lax.ppermute(high.astype(BF16), ("yhi", "core"), [(1, 3), (3, 1), (0, 0), (2, 2)])
    rows_grad = got.astype(F32) + jnp.where(first, low, more.astype(F32))
    with jax.named_scope("in_y"):
        here, there = after(in_grads[0:RANKS], (grads, got, more)), in_grads[RANKS:]
        in_grads = (here + flip(here, "ylo", 2, 1)) + (
            flip(there, "yhi", 2, 1) + flip(there, ("ylo", "yhi"), 4, 3)
        )
    g = [in_grads[i * RANK : (i + 1) * RANK] for i in range(3)]
    o = [grads[i * RANK : (i + 1) * RANK] for i in range(3)]
    return rows_grad.astype(BF16), g[0], o[0], g[1], o[1], o[2], g[2]


def solution(mesh):
    split = Mesh(mesh.devices.reshape(2, 4, 2, 8, 2), ("ylo", "x", "yhi", "z", "core"))
    dp, tensor = ("ylo", "x"), ("yhi", "z", "core")
    cols = P(None, tensor)
    return jax.shard_map(
        body,
        mesh=split,
        in_specs=(P(dp, tensor), P(dp, tensor), cols, cols, P(tensor, None), cols, cols, cols, cols, cols, cols),
        out_specs=(P(dp, tensor), cols, cols, cols, cols, cols, cols),
        check_vma=False,
    )
```
